256 devices in a mesh: dp: 16 (over y_hi, z), blk: 16 (over y_lo, x, core).
Axes of the slice: x: 4, y: 4 (y_hi: 2, y_lo: 2; y = y_hi * 2 + y_lo), z: 8, core: 2. Of those that a mesh axis runs over, the one named last changes fastest.
Arguments:
- feats: bfloat16 [65536, 1536], P(('dp', 'blk')), may hold values from -1 to 1
- head_weight: bfloat16 [1536, 1536], replicated, may hold values from -1.5 to 1.5
- text_raw: bfloat16 [65536, 1536], P(('dp', 'blk')), may hold values from -1 to 1
- log_temp: float32 [1], replicated, may hold values from 2.4 to 2.8
- bias: float32 [1], replicated, may hold values from -2 to -1
Outputs:
- text_grad: float32 [65536, 1536], P(('dp', 'blk'))
- weight_grad: float32 [1536, 1536], P('dp', 'blk')
The draws below stay inside these ranges and needn't reach their ends.
All inputs are finite; a program needn't handle non-finite values.
Results may differ from the reference program's by a relative error of at most 0.0016.
Values may be sent and summed in bfloat16 or wider, within the bound.
A program may use at most 128 MiB of HBM per device.

```python
import math
import jax
import jax.numpy as jnp
from jax import lax

E = 1536
F = 1536
B_DEV = 256
GROUP = 4096
ROWS = 65536
N_DP = 16
N_BLK = 16


def shared_base(key, share):
    id_key, center_key, own_key = jax.random.split(key, 3)
    clusters = max(GROUP // 16, 2)
    cluster_ids = jax.random.randint(id_key, (ROWS,), 0, clusters)
    owners = jnp.arange(ROWS, dtype=jnp.int32) // GROUP
    centers = jax.random.normal(center_key, (N_DP, clusters, F), jnp.float32)
    own_part = jax.random.normal(own_key, (ROWS, F), jnp.float32)
    return math.sqrt(share) * centers[owners, cluster_ids] + math.sqrt(1.0 - share) * own_part


def draw_feats(key, part):
    share = 0.5
    base = shared_base(key, share)
    key = jax.random.fold_in(key, 11)
    pair_key = jax.random.fold_in(key, 0)
    blocks = ROWS // B_DEV
    pairing = jax.random.permutation(pair_key, blocks)
    width = max(F // blocks, 1)
    starts = pairing[jnp.arange(ROWS, dtype=jnp.int32) // B_DEV] * F // blocks
    columns = jnp.arange(F, dtype=jnp.int32)
    spiked = (columns[None, :] >= starts[:, None]) & (columns[None, :] < starts[:, None] + width)
    values = base * jnp.where(spiked, 4.0, 1.0)
    return jnp.clip(0.0255 * values, -1.0, 1.0).astype(jnp.bfloat16)


def draw_text_raw(key, part):
    share = 0.5
    base = shared_base(key, share)
    key = jax.random.fold_in(key, 23)
    noise_key = jax.random.fold_in(key, 0)
    align = 0.8
    noise = jax.random.normal(noise_key, (ROWS, E), jnp.float32)
    values = align * base + math.sqrt(1.0 - align * align) * noise
    return jnp.clip(0.0255 * values, -1.0, 1.0).astype(jnp.bfloat16)


def draw_head_weight(key, part):
    key = jax.random.fold_in(key, 37)
    gain_key, noise_key = jax.random.split(key, 2)
    gains = jax.random.uniform(gain_key, (F,), jnp.float32, 0.8, 1.2)
    noise = jax.random.normal(noise_key, (F, E), jnp.float32) * (0.5 / math.sqrt(F))
    diagonal = jnp.arange(F, dtype=jnp.int32)[:, None] == jnp.arange(E, dtype=jnp.int32)[None, :]
    values = noise + jnp.where(diagonal, gains[:, None], 0.0)
    return jnp.clip(values, -1.5, 1.5).astype(jnp.bfloat16)


def setup_inputs(seed: int = 0) -> dict:
    streams_of = jax.random.split(jax.random.key(seed), 6)
    feats = draw_feats(jax.random.fold_in(streams_of[5], 71), 0)
    head_weight = draw_head_weight(jax.random.fold_in(streams_of[5], 71), 0)
    text_raw = draw_text_raw(jax.random.fold_in(streams_of[5], 71), 0)
    log_temp = jnp.clip(jax.random.uniform(streams_of[3], (1,), jnp.float32, 2.4, 2.8), 2.4, 2.8)
    bias = jnp.clip(jax.random.uniform(streams_of[4], (1,), jnp.float32, -2.0, -1.0), -2.0, -1.0)
    return dict(feats=feats, head_weight=head_weight, text_raw=text_raw, log_temp=log_temp, bias=bias)


loss_scale = 4096.0

def unit_rows(x):
    inv = lax.rsqrt(lax.optimization_barrier(jnp.sum(x * x, axis=-1, keepdims=True)) + 1e-06)
    return (x * inv, inv)

def back_rows(grad, unit32, inv):
    return (grad - unit32 * lax.optimization_barrier(jnp.sum(unit32 * grad, axis=-1, keepdims=True))) * inv

def reference(feats, head_weight, text_raw, log_temp, bias):
    scale = jnp.exp(log_temp[0])
    shift = bias[0]
    image_raw = jnp.dot(feats, head_weight, preferred_element_type=jnp.float32)
    img32, img_inv = unit_rows(image_raw)
    txt32, txt_inv = unit_rows(text_raw.astype(jnp.float32))
    image_unit = img32.astype(jnp.bfloat16)
    text_unit = txt32.astype(jnp.bfloat16)
    group = B_DEV * N_BLK
    factor = loss_scale / (N_DP * group)
    eye = jnp.eye(group, dtype=jnp.float32)

    def one_group(pair):
        left, right = pair
        logits = scale * lax.dot_general(left, right, (((1,), (1,)), ((), ())), preferred_element_type=jnp.float32) + shift
        coef = (factor * (jax.nn.sigmoid(logits) - eye)).astype(jnp.bfloat16)
        image_side = scale * jnp.dot(coef, right, preferred_element_type=jnp.float32)
        text_side = scale * lax.dot_general(coef, left, (((0,), (0,)), ((), ())), preferred_element_type=jnp.float32)
        return (image_side, text_side)
    image_side, text_side = lax.map(one_group, (image_unit.reshape(N_DP, group, E), text_unit.reshape(N_DP, group, E)))
    image_grad = back_rows(image_side.reshape(-1, E), img32, img_inv).astype(jnp.bfloat16)
    text_grad = back_rows(text_side.reshape(-1, E), txt32, txt_inv)
    weight_grad = lax.dot_general(feats, image_grad, (((0,), (0,)), ((), ())), preferred_element_type=jnp.float32)
    return (text_grad, weight_grad)
```

```python
import functools
import math

import jax
import jax.numpy as jnp
from jax import lax
from jax.experimental import pallas as pl
from jax.experimental.pallas import tpu as pltpu
from jax.sharding import PartitionSpec as P

MESH = pl.DeviceIdType.MESH
F32 = jnp.float32
BF16 = jnp.bfloat16
loss_scale = 4096.0

R = 256
E = 1536
F = 1536
H = 768
NX, NY, NZ = 4, 4, 8
OUT = 96

TEXT_CORE, TEXT_Y, TEXT_FWD = 0, 1, 2
XP1, XM1, XP2, XM2, XP3, XM3 = 3, 4, 5, 6, 7, 8
FT_CORE = 9
U_CORE = 13
CT_CORE = 17
G_CORE = 25
P_Y = 29
Z_RING = 33
Y_SUM = 57
X_SUM = 60
N_SEM = 64

P_CODE = 2.0**33
W_CODE = 2.0**4


def encode(v, s):
    v = v * s
    return (v * v * v).astype(BF16)


def decode(e, s):
    e = e.astype(F32)
    r = jnp.exp2(jnp.log2(jnp.maximum(jnp.abs(e), 1e-37)) * (1.0 / 3.0)) * (1.0 / s)
    return jnp.where(e > 0, r, jnp.where(e < 0, -r, 0.0))


def kernel(
    factor,
    lt_ref, bias_ref, feats_hbm, hw_hbm, text_hbm,
    tgrad_hbm, wgrad_ref,
    hw, ff, ft, u32, inv, uu, txr, tu, sw, ct, ctr, cfb, pp, yenc, yrecv,
    gall, ggr, zs, zr, zfin, zenc, yr2, ysum, xenc, xr3, scale_ref,
    load, ss, rs,
):
    dp, blk = lax.axis_index("dp"), lax.axis_index("blk")
    yh, z = dp // NZ, dp % NZ
    yl, x, c = blk // 8, (blk // 2) % NX, blk % 2
    y = yh * 2 + yl

    def dev(x, y, z, c):
        return ((y // 2) * NZ + z, (y % 2) * 8 + x * 2 + c)

    core = dev(x, y, z, 1 - c)
    xp, xm = dev((x + 1) % NX, y, z, c), dev((x + NX - 1) % NX, y, z, c)
    yp = dev(x, yh * 2 + 1 - yl, z, c)
    zp, zm = dev(x, y, (z + 1) % NZ, c), dev(x, y, (z + NZ - 1) % NZ, c)
    ys = [dev(x, (y + k) % NY, z, c) for k in (1, 2, 3)]
    xto = [(2 * c + k // 2, k % 2) for k in range(4)]
    xfrom = x // 2

    loads = [
        pltpu.make_async_copy(text_hbm, txr, load.at[0]),
        pltpu.make_async_copy(feats_hbm, ff.at[pl.ds(0, R)], load.at[1]),
        pltpu.make_async_copy(hw_hbm, hw, load.at[2]),
    ]
    for l in loads:
        l.start()
    bar = pltpu.get_barrier_semaphore()
    for d in [core, xp, xm, zp, zm] + ys:
        pl.semaphore_signal(bar, inc=1, device_id=d, device_id_type=MESH)
    for k in range(NX):
        @pl.when(jnp.logical_not((k == x) & (c == xfrom)))
        def _():
            pl.semaphore_signal(bar, inc=1, device_id=dev(k, y, z, xfrom), device_id_type=MESH)

    scale_ref[...] = jnp.exp(jnp.full((8, 128), lt_ref[0], F32))

    def scale():
        return scale_ref[0:1, 0:1]

    shift = bias_ref[0]

    def norm_text(i, _):
        rows = pl.ds(pl.multiple_of(i * 64, 64), 64)
        t = txr[rows, :].astype(F32)
        ti = lax.rsqrt(jnp.sum(t * t, axis=-1, keepdims=True) + 1e-06)
        tu[pl.ds(pl.multiple_of(c * R + i * 64, 64), 64), :] = (t * ti).astype(BF16)
        return 0

    loads[0].wait()
    lax.fori_loop(0, R // 64, norm_text, 0)

    pl.semaphore_wait(bar, 8 + 4 - jnp.where(c == xfrom, 1, 0))

    sent = []

    def send(src, dst, i, d, j=None):
        cp = pltpu.make_async_remote_copy(
            src, dst, ss.at[i], rs.at[i if j is None else j], device_id=d, device_id_type=MESH
        )
        cp.start()
        sent.append(cp)
        return cp

    trow = pl.ds(pl.multiple_of(c * R, R), R)
    tother = pl.ds(pl.multiple_of(2 * R + c * R, R), R)
    loads[1].wait()
    lo, hi = pl.ds(0, 128), pl.ds(128, 128)

    def half(b, k):
        return pl.ds(b * R + k * 128, 128)

    xp1 = send(ff.at[lo], ff.at[half(1, 0)], XP1, xp)
    xm1 = send(ff.at[hi], ff.at[half(1, 1)], XM1, xm)
    t_y = send(tu.at[trow], tu.at[tother], TEXT_Y, yp)
    t_core = send(tu.at[trow], tu.at[trow], TEXT_CORE, core)
    xp2 = send(ff.at[hi], ff.at[half(2, 0)], XP2, xp)
    xm2 = send(ff.at[lo], ff.at[half(2, 1)], XM2, xm)
    loads[2].wait()

    def rows_of(b, n=R):
        return pl.ds(pl.multiple_of(b * R, R), n)

    ft_cp, u_cp, ct_cp, g_cp = {}, {}, {}, {}

    def unit(b):
        rows = pl.ds(b * R, R)

        def raw(n, _):
            cols = pl.ds(pl.multiple_of(n * 256, 256), 256)
            u32[rows, cols] = jnp.dot(ff[rows, :], hw[:, cols], preferred_element_type=F32)
            return 0

        lax.fori_loop(0, 6, raw, 0)

        def norm(i, _):
            r = pl.ds(pl.multiple_of(b * R + i * 64, 64), 64)
            v = u32[r, :]
            iv = lax.rsqrt(jnp.sum(v * v, axis=-1, keepdims=True) + 1e-06)
            v = v * iv
            inv[r, :] = iv
            u32[r, :] = v
            uu[pl.ds(pl.multiple_of(b * R + i * 64, 64), 64), :] = v.astype(BF16)
            return 0

        lax.fori_loop(0, 4, norm, 0)
        u_cp[b] = send(uu.at[rows], uu.at[pl.ds(4 * R + b * R, R)], U_CORE + b, core)

    def transpose(b):
        rows = pl.ds(b * R, R)

        def tr(n, _):
            cols = pl.ds(pl.multiple_of(n * 256, 256), 256)
            ft[cols, pl.ds(b * R, R)] = ff[rows, cols].T
            return 0

        lax.fori_loop(0, 6, tr, 0)
        ft_cp[b] = send(
            ft.at[:, pl.ds(b * R, R)], ft.at[:, pl.ds(4 * R + b * R, R)], FT_CORE + b, core
        )

    def piece(b, h):
        rows = rows_of(b)
        for k in range(2):
            trows = pl.ds((2 * h + k) * R, R)
            logits = lax.dot_general(
                uu[rows, :], tu[trows, :], (((1,), (1,)), ((), ())), preferred_element_type=F32
            )
            logits = scale() * logits + shift
            p = jax.nn.sigmoid(logits)
            if h == 0 and isinstance(b, int) and b == 0:
                i = lax.broadcasted_iota(jnp.int32, p.shape, 0)
                j = lax.broadcasted_iota(jnp.int32, p.shape, 1)
                p = p - jnp.where((i == j) & (c == k), 1.0, 0.0)
            cf = (factor * p).astype(BF16)
            cfb[:, pl.ds(k * R, R)] = cf
            ct[b, h, k] = cf.T

    def exchange(b, h):
        ct_cp[b, h] = send(ct.at[b, h, 1 - c], ctr.at[b, h], CT_CORE + 2 * b + h, core)

    def side(b, h, first):
        rows2 = pl.ds(2 * h * R, 2 * R)

        def tile(n, _):
            cols = pl.ds(pl.multiple_of(n * 256, 256), 256)
            r = pl.ds(pl.multiple_of((n // 3) * 1024 + b * R, R), R)
            cc = pl.ds(pl.multiple_of((n % 3) * 256, 256), 256)
            v = jnp.dot(cfb[...], tu[rows2, cols], preferred_element_type=F32)
            sw[r, cc] = v if first else sw[r, cc] + v
            return 0

        lax.fori_loop(0, 6, tile, 0)

    def text_side(b, h, first):
        def tile(n, _):
            cols = pl.ds(pl.multiple_of(n * 256, 256), 256)
            v = jnp.dot(ct[b, h, c], uu[pl.ds(b * R, R), cols], preferred_element_type=F32)
            v = v + jnp.dot(ctr[b, h], uu[pl.ds(4 * R + b * R, R), cols], preferred_element_type=F32)
            pp[h, :, cols] = v if first else pp[h, :, cols] + v
            return 0

        lax.fori_loop(0, 6, tile, 0)

    unit(0)
    t_core.wait_recv()
    piece(0, 0)
    exchange(0, 0)
    side(0, 0, True)
    transpose(0)
    xp1.wait_recv()
    xp3 = send(ff.at[half(1, 0)], ff.at[half(3, 0)], XP3, xp)
    xm1.wait_recv()
    xm3 = send(ff.at[half(1, 1)], ff.at[half(3, 1)], XM3, xm)
    unit(1)
    piece(1, 0)
    exchange(1, 0)
    side(1, 0, True)
    u_cp[0].wait_recv()
    ct_cp[0, 0].wait_recv()
    text_side(0, 0, True)
    transpose(1)
    t_y.wait_recv()
    t_fwd = send(tu.at[tother], tu.at[tother], TEXT_FWD, core)
    xp2.wait_recv()
    xm2.wait_recv()
    unit(2)
    u_cp[1].wait_recv()
    ct_cp[1, 0].wait_recv()
    text_side(1, 0, False)
    piece(2, 0)
    exchange(2, 0)
    side(2, 0, True)
    t_fwd.wait_recv()
    for b in range(3):
        piece(b, 1)
        exchange(b, 1)
        side(b, 1, False)
        if b == 0:
            u_cp[2].wait_recv()
            ct_cp[2, 0].wait_recv()
            text_side(2, 0, False)
        else:
            ct_cp[b - 1, 1].wait_recv()
            text_side(b - 1, 1, b == 1)
    transpose(2)
    xp3.wait_recv()
    xm3.wait_recv()
    unit(3)
    piece(3, 1)
    exchange(3, 1)
    ct_cp[2, 1].wait_recv()
    text_side(2, 1, False)
    u_cp[3].wait_recv()
    ct_cp[3, 1].wait_recv()
    text_side(3, 1, False)
    p_cp = []
    for i in range(4):
        r = pl.ds(i * 64, 64)
        yenc[r, :] = encode(pp[1, r, :], P_CODE)
        p_cp.append(send(yenc.at[r], yrecv.at[r], P_Y + i, yp))
    side(3, 1, True)
    piece(3, 0)
    exchange(3, 0)
    side(3, 0, False)
    transpose(3)

    def image_grad(b):
        def chunk(i, _):
            r0 = b * R + i * 64
            r = pl.ds(pl.multiple_of(r0, 64), 64)
            rl = pl.ds(pl.multiple_of(1024 + r0, 64), 64)
            s = scale()
            g0, g1 = s * sw[r, :], s * sw[rl, :]
            v0, v1 = u32[r, pl.ds(0, H)], u32[r, pl.ds(H, H)]
            d = jnp.sum(v0 * g0, axis=-1, keepdims=True) + jnp.sum(v1 * g1, axis=-1, keepdims=True)
            iv = inv[r, :]
            g0 = ((g0 - v0 * d) * iv).astype(BF16)
            g1 = ((g1 - v1 * d) * iv).astype(BF16)
            for k in range(2):
                gall[k, r, pl.ds(0, 384)] = g0[:, k * 384 : k * 384 + 384]
                gall[k, r, pl.ds(384, 384)] = g1[:, k * 384 : k * 384 + 384]
            return 0

        lax.fori_loop(0, 4, chunk, 0)
        rows = pl.ds(b * R, R)
        g_cp[b] = send(gall.at[1 - c, rows], ggr.at[rows], G_CORE + b, core)

    for b in range(4):
        image_grad(b)
    ct_cp[3, 0].wait_recv()
    text_side(3, 0, False)
    for b in range(4):
        ft_cp[b].wait_recv()
        g_cp[b].wait_recv()

    def weight(n):
        cols = pl.ds(n * 256, 256)

        def tile(m, _):
            r = pl.ds(pl.multiple_of(m * 256, 256), 256)
            v = jnp.dot(ft[r, pl.ds(0, 1024)], gall[c, :, cols], preferred_element_type=F32)
            sw[r, cols] = v + jnp.dot(ft[r, pl.ds(1024, 1024)], ggr[:, cols], preferred_element_type=F32)
            return 0

        lax.fori_loop(0, 6, tile, 0)

    def own(n, zz, k):
        return sw[pl.ds(pl.multiple_of(k * H + zz * OUT, 32), OUT), pl.ds(n * 256, 256)]

    ring = {}

    def step(n, s):
        cps = []
        for d in range(2):
            zz = (z + (4 - s if d == 0 else NZ - 4 + s)) % NZ
            i = (n * 2 + d) * 4 + s
            if s:
                ring[n, s - 1][d].wait_recv()
            for k in range(2):
                if s == 0 and k != d:
                    continue
                v = own(n, zz, k)
                if s > 1 or (s == 1 and k == d):
                    v = v + decode(zr[i - 1, pl.ds(k * OUT, OUT), :], W_CODE)
                zs[i, pl.ds(k * OUT, OUT), :] = encode(v, W_CODE)
            r = pl.ds(d * OUT, OUT) if s == 0 else pl.ds(0, 2 * OUT)
            cps.append(send(zs.at[i, r], zr.at[i, r], Z_RING + i, zp if d == 0 else zm))
        ring[n, s] = cps

    def final(n):
        for d in range(2):
            ring[n, 3][d].wait_recv()
        for k in range(2):
            r = pl.ds(k * OUT, OUT)
            v = own(n, z, k)
            for d in range(2):
                v = v + decode(zr[(n * 2 + d) * 4 + 3, r, :], W_CODE)
            zfin[r, pl.ds(n * 256, 256)] = v
            zenc[r, pl.ds(n * 256, 256)] = encode(v, W_CODE)

    out_cp = []

    def text_out(i):
        p_cp[i].wait_recv()
        r = pl.ds(i * 64, 64)
        t = txr[r, :].astype(F32)
        ti = lax.rsqrt(jnp.sum(t * t, axis=-1, keepdims=True) + 1e-06)
        t = t * ti
        g = scale() * (pp[0, r, :] + decode(yrecv[r, :], P_CODE))
        pp[0, r, :] = (g - t * jnp.sum(t * g, axis=-1, keepdims=True)) * ti
        cp = pltpu.make_async_copy(pp.at[0, r], tgrad_hbm.at[r], load.at[3 + i])
        cp.start()
        out_cp.append(cp)

    weight(0)
    step(0, 0)
    weight(1)
    step(1, 0)
    step(0, 1)
    weight(2)
    step(2, 0)
    step(1, 1)
    step(0, 2)
    text_out(0)
    step(2, 1)
    text_out(1)
    step(1, 2)
    step(0, 3)
    text_out(2)
    step(2, 2)
    text_out(3)
    step(1, 3)
    final(0)
    step(2, 3)
    final(1)
    final(2)

    def zslice(yy):
        return (
            pl.ds(pl.multiple_of((yy // 2) * OUT, 32), OUT),
            pl.ds(pl.multiple_of((yy % 2) * 384, 128), 384),
        )

    y_cp = []
    for k in range(3):
        r, cc = zslice((y + k + 1) % NY)
        y_cp.append(send(zenc.at[r, cc], yr2.at[k], Y_SUM + k, ys[k]))
    r, cc = zslice(y)
    v = zfin[r, cc]
    for k in range(3):
        y_cp[k].wait_recv()
        v = v + decode(yr2[k], W_CODE)
    ysum[...] = v
    xenc[...] = encode(v, W_CODE)

    cps = []
    for k in range(4):
        xx, kc = xto[k]
        cols = pl.ds(128 * (k // 2), 256)
        cp = pltpu.make_async_remote_copy(
            xenc.at[:, cols], xr3.at[x], ss.at[X_SUM + k], rs.at[X_SUM + x],
            device_id=dev(xx, y, z, kc), device_id_type=MESH,
        )
        mine = (xx == x) & (kc == c)

        @pl.when(jnp.logical_not(mine))
        def _():
            cp.start()

        @pl.when(mine)
        def _():
            xr3[x] = xenc[:, cols]

        cps.append((cp, mine))
    for k in range(4):
        @pl.when(jnp.logical_not((k == x) & (c == xfrom)))
        def _():
            pltpu.make_async_remote_copy(
                xenc.at[:, pl.ds(0, 256)], xr3.at[k], ss.at[X_SUM + k], rs.at[X_SUM + k],
                device_id=core, device_id_type=MESH,
            ).wait_recv()

    v = decode(xr3[0], W_CODE)
    for k in range(1, 4):
        v = v + decode(xr3[k], W_CODE)
    mine = 2 * (x % 2) + c
    out = v[:, :OUT]
    for k, off in ((1, 96), (2, 64), (3, 160)):
        out = jnp.where(mine == k, pltpu.roll(v, 256 - off, 1)[:, :OUT], out)
    wgrad_ref[...] = out

    for cp in sent:
        cp.wait_send()
    for cp, mine in cps:
        @pl.when(jnp.logical_not(mine))
        def _():
            cp.wait_send()
    for cp in out_cp:
        cp.wait()


def local(feats, head_weight, text_raw, log_temp, bias):
    rows = feats.shape[0]
    factor = loss_scale / (lax.axis_size("dp") * rows * lax.axis_size("blk"))
    vmem = pltpu.VMEM
    scratch = [
        vmem((F, E), BF16),
        vmem((4 * R, F), BF16),
        vmem((F, 8 * R), BF16),
        vmem((4 * R, E), F32),
        vmem((4 * R, 1), F32),
        vmem((8 * R, E), BF16),
        vmem((R, E), BF16),
        vmem((4 * R, E), BF16),
        vmem((8 * R, H), F32),
        vmem((4, 2, 2, R, R), BF16),
        vmem((4, 2, R, R), BF16),
        vmem((R, 2 * R), BF16),
        vmem((2, R, E), F32),
        vmem((R, E), BF16),
        vmem((R, E), BF16),
        vmem((2, 4 * R, H), BF16),
        vmem((4 * R, H), BF16),
        vmem((24, 2 * OUT, 256), BF16),
        vmem((24, 2 * OUT, 256), BF16),
        vmem((2 * OUT, H), F32),
        vmem((2 * OUT, H), BF16),
        vmem((3, OUT, 384), BF16),
        vmem((OUT, 384), F32),
        vmem((OUT, 384), BF16),
        vmem((4, OUT, 256), BF16),
        vmem((8, 128), F32),
        pltpu.SemaphoreType.DMA((7,)),
        pltpu.SemaphoreType.DMA((N_SEM,)),
        pltpu.SemaphoreType.DMA((N_SEM,)),
    ]
    anyspec = pl.BlockSpec(memory_space=pl.ANY)
    smem = pl.BlockSpec(memory_space=pltpu.SMEM)
    return pl.pallas_call(
        functools.partial(kernel, factor),
        out_shape=(
            jax.ShapeDtypeStruct((R, E), F32),
            jax.ShapeDtypeStruct((OUT, OUT), F32),
        ),
        in_specs=[smem, smem, anyspec, anyspec, anyspec],
        out_specs=(anyspec, pl.BlockSpec(memory_space=pltpu.VMEM)),
        scratch_shapes=scratch,
        compiler_params=pltpu.CompilerParams(
            collective_id=0, has_side_effects=True, vmem_limit_bytes=63 * 1024 * 1024
        ),
        cost_estimate=pl.CostEstimate(
            flops=20_000_000_000, bytes_accessed=8_000_000, transcendentals=4_000_000
        ),
    )(log_temp, bias, feats, head_weight, text_raw)


def solution(mesh):
    return jax.shard_map(
        local,
        mesh=mesh,
        in_specs=(P(("dp", "blk"), None), P(), P(("dp", "blk"), None), P(), P()),
        out_specs=(P(("dp", "blk"), None), P("dp", "blk")),
        check_vma=False,
    )
```

```python
import functools
import math

import jax
import jax.numpy as jnp
from jax import lax
from jax.experimental import pallas as pl
from jax.experimental.pallas import tpu as pltpu
from jax.sharding import PartitionSpec as P

MESH = pl.DeviceIdType.MESH
F32 = jnp.float32
BF16 = jnp.bfloat16
loss_scale = 4096.0

R = 256
E = 1536
F = 1536
H = 768
NX, NY, NZ = 4, 4, 8
OUT = 96

TEXT_CORE, TEXT_Y, TEXT_FWD = 0, 1, 2
XP1, XM1, XP2, XM2, XP3, XM3 = 3, 4, 5, 6, 7, 8
FT_CORE = 9
U_CORE = 13
CT_CORE = 17
G_CORE = 25
P_Y = 29
Z_RING = 33
Y_SUM = 57
X_SUM = 66
N_SEM = 74

P_CODE = 2.0**33
W_CODE = 2.0**4


def encode(v, s):
    v = v * s
    return (v * v * v).astype(BF16)


def decode(e, s):
    e = e.astype(F32)
    r = jnp.exp2(jnp.log2(jnp.maximum(jnp.abs(e), 1e-37)) * (1.0 / 3.0)) * (1.0 / s)
    return jnp.where(e > 0, r, jnp.where(e < 0, -r, 0.0))


def kernel(
    factor,
    lt_ref, bias_ref, feats_hbm, hw_hbm, text_hbm,
    tgrad_hbm, wgrad_ref,
    hw, ff, ft, u32, inv, uu, txr, tu, sw, pc, cs, cf, pp, yenc, yrecv,
    gg, gs, zs, zr, zfin, zenc, yr2, xenc, xr3, scale_ref,
    load, ss, rs,
):
    dp, blk = lax.axis_index("dp"), lax.axis_index("blk")
    yh, z = dp // NZ, dp % NZ
    yl, x, c = blk // 8, (blk // 2) % NX, blk % 2
    y = yh * 2 + yl

    def dev(x, y, z, c):
        return ((y // 2) * NZ + z, (y % 2) * 8 + x * 2 + c)

    core = dev(x, y, z, 1 - c)
    xp, xm = dev((x + 1) % NX, y, z, c), dev((x + NX - 1) % NX, y, z, c)
    yp = dev(x, yh * 2 + 1 - yl, z, c)
    zp, zm = dev(x, y, (z + 1) % NZ, c), dev(x, y, (z + NZ - 1) % NZ, c)
    ys = [dev(x, (y + k) % NY, z, c) for k in (1, 2, 3)]
    xto = [(2 * c + k // 2, k % 2) for k in range(4)]
    xfrom = x // 2

    loads = [
        pltpu.make_async_copy(text_hbm, txr, load.at[0]),
        pltpu.make_async_copy(feats_hbm, ff.at[pl.ds(0, R)], load.at[1]),
        pltpu.make_async_copy(hw_hbm, hw, load.at[2]),
    ]
    for l in loads:
        l.start()
    bar = pltpu.get_barrier_semaphore()
    for d in [core, xp, xm, zp, zm] + ys:
        pl.semaphore_signal(bar, inc=1, device_id=d, device_id_type=MESH)
    for k in range(NX):
        @pl.when(jnp.logical_not((k == x) & (c == xfrom)))
        def _():
            pl.semaphore_signal(bar, inc=1, device_id=dev(k, y, z, xfrom), device_id_type=MESH)

    scale_ref[...] = jnp.exp(jnp.full((8, 128), lt_ref[0], F32))

    def scale():
        return scale_ref[0:1, 0:1]

    shift = bias_ref[0]

    def norm_text(i, _):
        rows = pl.ds(pl.multiple_of(i * 64, 64), 64)
        t = txr[rows, :].astype(F32)
        ti = lax.rsqrt(jnp.sum(t * t, axis=-1, keepdims=True) + 1e-06)
        tu[pl.ds(pl.multiple_of(c * R + i * 64, 64), 64), :] = (t * ti).astype(BF16)
        return 0

    loads[0].wait()
    lax.fori_loop(0, R // 64, norm_text, 0)

    pl.semaphore_wait(bar, 8 + 4 - jnp.where(c == xfrom, 1, 0))

    sent = []

    def send(src, dst, i, d, j=None):
        cp = pltpu.make_async_remote_copy(
            src, dst, ss.at[i], rs.at[i if j is None else j], device_id=d, device_id_type=MESH
        )
        cp.start()
        sent.append(cp)
        return cp

    trow = pl.ds(pl.multiple_of(c * R, R), R)
    tother = pl.ds(pl.multiple_of(2 * R + c * R, R), R)
    loads[1].wait()
    lo, hi = pl.ds(0, 128), pl.ds(128, 128)

    def half(b, k):
        return pl.ds(b * R + k * 128, 128)

    xp1 = send(ff.at[lo], ff.at[half(1, 0)], XP1, xp)
    xm1 = send(ff.at[hi], ff.at[half(1, 1)], XM1, xm)
    t_y = send(tu.at[trow], tu.at[tother], TEXT_Y, yp)
    t_core = send(tu.at[trow], tu.at[trow], TEXT_CORE, core)
    xp2 = send(ff.at[hi], ff.at[half(2, 0)], XP2, xp)
    xm2 = send(ff.at[lo], ff.at[half(2, 1)], XM2, xm)
    loads[2].wait()

    ft_cp, u_cp, ct_cp, g_cp = {}, {}, {}, {}

    def unit(b):
        rows = pl.ds(b * R, R)
        u32[rows, :] = jnp.dot(ff[rows, :], hw[...], preferred_element_type=F32)

        def norm(i, _):
            r = pl.ds(pl.multiple_of(b * R + i * 64, 64), 64)
            v = u32[r, :]
            iv = lax.rsqrt(jnp.sum(v * v, axis=-1, keepdims=True) + 1e-06)
            v = v * iv
            inv[r, :] = iv
            u32[r, :] = v
            uu[r, :] = v.astype(BF16)
            return 0

        lax.fori_loop(0, 4, norm, 0)
        u_cp[b] = send(uu.at[rows], uu.at[pl.ds(4 * R + b * R, R)], U_CORE + b, core)

        def tr(n, _):
            cols = pl.ds(pl.multiple_of(n * 256, 256), 256)
            ft[cols, pl.ds(b * R, R)] = ff[rows, cols].T
            return 0

        lax.fori_loop(0, 6, tr, 0)
        ft_cp[b] = send(
            ft.at[:, pl.ds(b * R, R)], ft.at[:, pl.ds(4 * R + b * R, R)], FT_CORE + b, core
        )

    def coefs(b, n, h):
        rows = pl.ds(b * R, n * R)
        logits = lax.dot_general(
            uu[rows, :], tu[pl.ds(2 * h * R, 2 * R), :], (((1,), (1,)), ((), ())),
            preferred_element_type=F32,
        )
        p = jax.nn.sigmoid(scale() * logits + shift)
        if h == 0 and b == 0:
            i = lax.broadcasted_iota(jnp.int32, p.shape, 0)
            j = lax.broadcasted_iota(jnp.int32, p.shape, 1)
            p = p - jnp.where(i + c * R == j, 1.0, 0.0)
        p = (factor * p).astype(BF16)
        cf[rows, pl.ds(2 * h * R, 2 * R)] = p
        t0, t1 = p[:, :R].T, p[:, R:].T
        pc[h, :, rows] = jnp.where(c == 0, t0, t1)
        cs[h, :, rows] = jnp.where(c == 0, t1, t0)
        ct_cp[b, h] = send(
            cs.at[h, :, rows], pc.at[h, :, pl.ds(4 * R + b * R, n * R)], CT_CORE + 2 * b + h, core
        )

    def image_grad(b, n):
        rows = pl.ds(b * R, n * R)
        for k in range(2):
            sw[pl.ds(k * H, n * R), :] = jnp.dot(
                cf[rows, :], tu[:, pl.ds(k * H, H)], preferred_element_type=F32
            )

        def chunk(i, _):
            r = pl.ds(pl.multiple_of(b * R + i * 64, 64), 64)
            s = scale()
            g0 = s * sw[pl.ds(pl.multiple_of(i * 64, 64), 64), :]
            g1 = s * sw[pl.ds(pl.multiple_of(H + i * 64, 64), 64), :]
            v0, v1 = u32[r, pl.ds(0, H)], u32[r, pl.ds(H, H)]
            d = jnp.sum(v0 * g0 + v1 * g1, axis=-1, keepdims=True)
            iv = inv[r, :]
            g = [((g0 - v0 * d) * iv).astype(BF16), ((g1 - v1 * d) * iv).astype(BF16)]
            for t in range(3):
                for l in range(2):
                    a0, a1 = g[l][:, t * 128 : t * 128 + 128], g[l][:, 384 + t * 128 : 512 + t * 128]
                    cols = pl.ds((2 * t + l) * 128, 128)
                    gg[r, cols] = jnp.where(c == 0, a0, a1)
                    gs[r, cols] = jnp.where(c == 0, a1, a0)
            return 0

        lax.fori_loop(0, 4 * n, chunk, 0)
        g_cp[b] = send(gs.at[rows], gg.at[pl.ds(4 * R + b * R, n * R)], G_CORE + b, core)

    unit(0)
    t_core.wait_recv()
    coefs(0, 1, 0)
    xp1.wait_recv()
    xp3 = send(ff.at[half(1, 0)], ff.at[half(3, 0)], XP3, xp)
    xm1.wait_recv()
    xm3 = send(ff.at[half(1, 1)], ff.at[half(3, 1)], XM3, xm)
    unit(1)
    coefs(1, 1, 0)
    t_y.wait_recv()
    t_fwd = send(tu.at[tother], tu.at[tother], TEXT_FWD, core)
    xp2.wait_recv()
    xm2.wait_recv()
    unit(2)
    coefs(2, 1, 0)
    t_fwd.wait_recv()
    coefs(0, 3, 1)
    image_grad(0, 3)
    xp3.wait_recv()
    xm3.wait_recv()
    unit(3)
    coefs(3, 1, 0)
    coefs(3, 1, 1)
    image_grad(3, 1)
    for b in range(4):
        ft_cp[b].wait_recv()
    g_cp[0].wait_recv()
    g_cp[3].wait_recv()

    def weight(n):
        cols = pl.ds(n * 256, 256)
        sw[:, cols] = jnp.dot(ft[...], gg[:, cols], preferred_element_type=F32)

    def own(n, zz, k):
        return sw[pl.ds(pl.multiple_of(k * H + zz * OUT, 32), OUT), pl.ds(n * 256, 256)]

    ring = {}

    def step(n, s):
        cps = []
        for d in range(2):
            zz = (z + (4 - s if d == 0 else NZ - 4 + s)) % NZ
            i = (n * 2 + d) * 4 + s
            if s:
                ring[n, s - 1][d].wait_recv()
            for k in range(2):
                if s == 0 and k != d:
                    continue
                v = own(n, zz, k)
                if s > 1 or (s == 1 and k == d):
                    v = v + decode(zr[i - 1, pl.ds(k * OUT, OUT), :], W_CODE)
                zs[i, pl.ds(k * OUT, OUT), :] = encode(v, W_CODE)
            r = pl.ds(d * OUT, OUT) if s == 0 else pl.ds(0, 2 * OUT)
            cps.append(send(zs.at[i, r], zr.at[i, r], Z_RING + i, zp if d == 0 else zm))
        ring[n, s] = cps

    y_cp = {}

    def final(n):
        for d in range(2):
            ring[n, 3][d].wait_recv()
        cols = pl.ds(n * 256, 256)
        for k in range(2):
            r = pl.ds(k * OUT, OUT)
            v = own(n, z, k)
            for d in range(2):
                v = v + decode(zr[(n * 2 + d) * 4 + 3, r, :], W_CODE)
            zfin[r, cols] = v
            zenc[r, cols] = encode(v, W_CODE)
        for k in range(3):
            r, cc = yslice(n, (y + k + 1) % NY)
            y_cp[n, k] = send(zenc.at[r, cc], yr2.at[n, k], Y_SUM + 3 * n + k, ys[k])

    def yslice(n, yy):
        return (
            pl.ds(pl.multiple_of((yy // 2) * OUT, 32), OUT),
            pl.ds(pl.multiple_of(n * 256 + (yy % 2) * 128, 128), 128),
        )

    x_cp = []

    def over_x(n):
        r, cc = yslice(n, y)
        v = zfin[r, cc]
        for k in range(3):
            y_cp[n, k].wait_recv()
            v = v + decode(yr2[n, k], W_CODE)
        xenc[n] = encode(v, W_CODE)
        for k in range(4):
            j = n - k // 2
            if j not in (0, 1):
                continue
            xx, kc = xto[k]
            cols = pl.ds(j * 128, 128)
            cp = pltpu.make_async_remote_copy(
                xenc.at[n], xr3.at[x, :, cols], ss.at[X_SUM + len(x_cp)], rs.at[X_SUM + 4 * j + x],
                device_id=dev(xx, y, z, kc), device_id_type=MESH,
            )
            mine = (xx == x) & (kc == c)

            @pl.when(jnp.logical_not(mine))
            def _():
                cp.start()

            @pl.when(mine)
            def _():
                xr3[x, :, cols] = xenc[n]

            x_cp.append((cp, mine))

    out_cp = []

    def text_side(h):
        pp[h] = jnp.dot(pc[h], uu[...], preferred_element_type=F32)

    p_cp = []

    def text_send():
        for i in range(4):
            r = pl.ds(i * 64, 64)
            yenc[r, :] = encode(pp[1, r, :], P_CODE)
            p_cp.append(send(yenc.at[r], yrecv.at[r], P_Y + i, yp))

    def text_out(i):
        p_cp[i].wait_recv()
        r = pl.ds(i * 64, 64)
        t = txr[r, :].astype(F32)
        ti = lax.rsqrt(jnp.sum(t * t, axis=-1, keepdims=True) + 1e-06)
        t = t * ti
        g = scale() * (pp[0, r, :] + decode(yrecv[r, :], P_CODE))
        pp[0, r, :] = (g - t * jnp.sum(t * g, axis=-1, keepdims=True)) * ti
        cp = pltpu.make_async_copy(pp.at[0, r], tgrad_hbm.at[r], load.at[3 + i])
        cp.start()
        out_cp.append(cp)

    weight(0)
    step(0, 0)
    weight(1)
    step(1, 0)
    step(0, 1)
    weight(2)
    step(2, 0)
    step(1, 1)
    for b in range(4):
        u_cp[b].wait_recv()
    for key in ct_cp:
        ct_cp[key].wait_recv()
    text_side(1)
    text_send()
    step(2, 1)
    step(0, 2)
    text_side(0)
    step(1, 2)
    step(2, 2)
    step(0, 3)
    step(1, 3)
    step(2, 3)
    text_out(0)
    final(0)
    text_out(1)
    final(1)
    text_out(2)
    over_x(0)
    final(2)
    text_out(3)
    over_x(1)
    over_x(2)

    for j in range(2):
        for k in range(4):
            @pl.when(jnp.logical_not((k == x) & (c == xfrom)))
            def _():
                pltpu.make_async_remote_copy(
                    xenc.at[0], xr3.at[k, :, pl.ds(j * 128, 128)],
                    ss.at[X_SUM + 4 * j + k], rs.at[X_SUM + 4 * j + k],
                    device_id=core, device_id_type=MESH,
                ).wait_recv()

    v = decode(xr3[0], W_CODE)
    for k in range(1, 4):
        v = v + decode(xr3[k], W_CODE)
    mine = 2 * (x % 2) + c
    out = v[:, :OUT]
    for k, off in ((1, 96), (2, 64), (3, 160)):
        out = jnp.where(mine == k, pltpu.roll(v, 256 - off, 1)[:, :OUT], out)
    wgrad_ref[...] = out

    for cp in sent:
        cp.wait_send()
    for cp, mine in x_cp:
        @pl.when(jnp.logical_not(mine))
        def _():
            cp.wait_send()
    for cp in out_cp:
        cp.wait()


def local(feats, head_weight, text_raw, log_temp, bias):
    rows = feats.shape[0]
    factor = loss_scale / (lax.axis_size("dp") * rows * lax.axis_size("blk"))
    vmem = pltpu.VMEM
    scratch = [
        vmem((F, E), BF16),
        vmem((4 * R, F), BF16),
        vmem((F, 8 * R), BF16),
        vmem((4 * R, E), F32),
        vmem((4 * R, 1), F32),
        vmem((8 * R, E), BF16),
        vmem((R, E), BF16),
        vmem((4 * R, E), BF16),
        vmem((F, H), F32),
        vmem((2, R, 8 * R), BF16),
        vmem((2, R, 4 * R), BF16),
        vmem((4 * R, 4 * R), BF16),
        vmem((2, R, E), F32),
        vmem((R, E), BF16),
        vmem((R, E), BF16),
        vmem((8 * R, H), BF16),
        vmem((4 * R, H), BF16),
        vmem((24, 2 * OUT, 256), BF16),
        vmem((24, 2 * OUT, 256), BF16),
        vmem((2 * OUT, H), F32),
        vmem((2 * OUT, H), BF16),
        vmem((3, 3, OUT, 128), BF16),
        vmem((3, OUT, 128), BF16),
        vmem((4, OUT, 256), BF16),
        vmem((8, 128), F32),
        pltpu.SemaphoreType.DMA((7,)),
        pltpu.SemaphoreType.DMA((N_SEM,)),
        pltpu.SemaphoreType.DMA((N_SEM,)),
    ]
    anyspec = pl.BlockSpec(memory_space=pl.ANY)
    smem = pl.BlockSpec(memory_space=pltpu.SMEM)
    return pl.pallas_call(
        functools.partial(kernel, factor),
        out_shape=(
            jax.ShapeDtypeStruct((R, E), F32),
            jax.ShapeDtypeStruct((OUT, OUT), F32),
        ),
        in_specs=[smem, smem, anyspec, anyspec, anyspec],
        out_specs=(anyspec, pl.BlockSpec(memory_space=pltpu.VMEM)),
        scratch_shapes=scratch,
        compiler_params=pltpu.CompilerParams(
            collective_id=0, has_side_effects=True, vmem_limit_bytes=63 * 1024 * 1024
        ),
        cost_estimate=pl.CostEstimate(
            flops=20_000_000_000, bytes_accessed=8_000_000, transcendentals=4_000_000
        ),
    )(log_temp, bias, feats, head_weight, text_raw)


def solution(mesh):
    return jax.shard_map(
        local,
        mesh=mesh,
        in_specs=(P(("dp", "blk"), None), P(), P(("dp", "blk"), None), P(), P()),
        out_specs=(P(("dp", "blk"), None), P("dp", "blk")),
        check_vma=False,
    )
```

```python
import functools
import math

import jax
import jax.numpy as jnp
from jax import lax
from jax.experimental import pallas as pl
from jax.experimental.pallas import tpu as pltpu
from jax.sharding import PartitionSpec as P

MESH = pl.DeviceIdType.MESH
F32 = jnp.float32
BF16 = jnp.bfloat16
loss_scale = 4096.0

R = 256
E = 1536
F = 1536
H = 768
NX, NY, NZ = 4, 4, 8
OUT = 96

TEXT_CORE, TEXT_Y, TEXT_FWD = 0, 1, 2
XP1, XM1, XP2, XM2, XP3, XM3 = 3, 4, 5, 6, 7, 8
FT_CORE = 9
U_CORE = 13
CT_CORE = 17
G_CORE = 25
P_Y = 29
Z_RING = 33
Y_SUM = 57
X_SUM = 66
N_SEM = 74

P_CODE = 2.0**33
W_CODE = 2.0**4


def encode(v, s):
    v = v * s
    return (v * v * v).astype(BF16)


def decode(e, s):
    e = e.astype(F32)
    r = jnp.exp2(jnp.log2(jnp.maximum(jnp.abs(e), 1e-37)) * (1.0 / 3.0)) * (1.0 / s)
    return jnp.where(e > 0, r, jnp.where(e < 0, -r, 0.0))


def kernel(
    factor,
    lt_ref, bias_ref, feats_hbm, hw_hbm, text_hbm,
    tgrad_hbm, wgrad_ref,
    hw, ff, ft, u32, inv, uu, txr, tu, sw, pc, cs, cf, pp, yenc, yrecv,
    gg, gs, zs, zr, zfin, zenc, yr2, xenc, xr3, scale_ref,
    load, ss, rs,
):
    dp, blk = lax.axis_index("dp"), lax.axis_index("blk")
    yh, z = dp // NZ, dp % NZ
    yl, x, c = blk // 8, (blk // 2) % NX, blk % 2
    y = yh * 2 + yl

    def dev(x, y, z, c):
        return ((y // 2) * NZ + z, (y % 2) * 8 + x * 2 + c)

    core = dev(x, y, z, 1 - c)
    xp, xm = dev((x + 1) % NX, y, z, c), dev((x + NX - 1) % NX, y, z, c)
    yp = dev(x, yh * 2 + 1 - yl, z, c)
    zp, zm = dev(x, y, (z + 1) % NZ, c), dev(x, y, (z + NZ - 1) % NZ, c)
    ys = [dev(x, (y + k) % NY, z, c) for k in (1, 2, 3)]
    xto = [(2 * c + k // 2, k % 2) for k in range(4)]
    xfrom = x // 2

    loads = [
        pltpu.make_async_copy(text_hbm, txr, load.at[0]),
        pltpu.make_async_copy(feats_hbm, ff.at[pl.ds(0, R)], load.at[1]),
        pltpu.make_async_copy(hw_hbm, hw, load.at[2]),
    ]
    for l in loads:
        l.start()
    bar = pltpu.get_barrier_semaphore()
    for d in [core, xp, xm, zp, zm] + ys:
        pl.semaphore_signal(bar, inc=1, device_id=d, device_id_type=MESH)
    for k in range(NX):
        @pl.when(jnp.logical_not((k == x) & (c == xfrom)))
        def _():
            pl.semaphore_signal(bar, inc=1, device_id=dev(k, y, z, xfrom), device_id_type=MESH)

    scale_ref[...] = jnp.exp(jnp.full((8, 128), lt_ref[0], F32))

    def scale():
        return scale_ref[0:1, 0:1]

    shift = bias_ref[0]

    def norm_text(i, _):
        rows = pl.ds(pl.multiple_of(i * 64, 64), 64)
        t = txr[rows, :].astype(F32)
        ti = lax.rsqrt(jnp.sum(t * t, axis=-1, keepdims=True) + 1e-06)
        tu[pl.ds(pl.multiple_of(c * R + i * 64, 64), 64), :] = (t * ti).astype(BF16)
        return 0

    pl.semaphore_wait(bar, 8 + 4 - jnp.where(c == xfrom, 1, 0))

    sent = []

    def send(src, dst, i, d, j=None):
        cp = pltpu.make_async_remote_copy(
            src, dst, ss.at[i], rs.at[i if j is None else j], device_id=d, device_id_type=MESH
        )
        cp.start()
        sent.append(cp)
        return cp

    trow = pl.ds(pl.multiple_of(c * R, R), R)
    tother = pl.ds(pl.multiple_of(2 * R + c * R, R), R)
    loads[1].wait()
    lo, hi = pl.ds(0, 128), pl.ds(128, 128)

    def half(b, k):
        return pl.ds(b * R + k * 128, 128)

    xp1 = send(ff.at[lo], ff.at[half(1, 0)], XP1, xp)
    xm1 = send(ff.at[hi], ff.at[half(1, 1)], XM1, xm)
    xp2 = send(ff.at[hi], ff.at[half(2, 0)], XP2, xp)
    xm2 = send(ff.at[lo], ff.at[half(2, 1)], XM2, xm)
    loads[0].wait()
    lax.fori_loop(0, R // 64, norm_text, 0)
    t_y = send(tu.at[trow], tu.at[tother], TEXT_Y, yp)
    t_core = send(tu.at[trow], tu.at[trow], TEXT_CORE, core)
    loads[2].wait()

    ft_cp, u_cp, ct_cp, g_cp = {}, {}, {}, {}

    alone = pl.when(dp >= 0)

    def unit(b):
        rows = pl.ds(b * R, R)

        @alone
        def _():
            u32[rows, :] = jnp.dot(ff[rows, :], hw[...], preferred_element_type=F32)
            ft[:, rows] = ff[rows, :].T

        def norm(i, _):
            r = pl.ds(pl.multiple_of(b * R + i * 64, 64), 64)
            v = u32[r, :]
            iv = lax.rsqrt(jnp.sum(v * v, axis=-1, keepdims=True) + 1e-06)
            inv[r, :] = iv
            uu[r, :] = (v * iv).astype(BF16)
            return 0

        lax.fori_loop(0, 4, norm, 0)
        u_cp[b] = send(uu.at[rows], uu.at[pl.ds(4 * R + b * R, R)], U_CORE + b, core)
        ft_cp[b] = send(
            ft.at[:, rows], ft.at[:, pl.ds(4 * R + b * R, R)], FT_CORE + b, core
        )

    def coefs(b, n, h):
        rows = pl.ds(b * R, n * R)

        @alone
        def _():
            logits = lax.dot_general(
                uu[rows, :], tu[pl.ds(2 * h * R, 2 * R), :], (((1,), (1,)), ((), ())),
                preferred_element_type=F32,
            )
            p = jax.nn.sigmoid(scale() * logits + shift)
            if h == 0 and b == 0:
                i = lax.broadcasted_iota(jnp.int32, p.shape, 0)
                j = lax.broadcasted_iota(jnp.int32, p.shape, 1)
                p = p - jnp.where(i + c * R == j, 1.0, 0.0)
            p = (factor * p).astype(BF16)
            cf[rows, pl.ds(2 * h * R, 2 * R)] = p
            t0, t1 = p[:, :R].T, p[:, R:].T
            pc[h, :, rows] = jnp.where(c == 0, t0, t1)
            cs[h, :, rows] = jnp.where(c == 0, t1, t0)

        ct_cp[b, h] = send(
            cs.at[h, :, rows], pc.at[h, :, pl.ds(4 * R + b * R, n * R)], CT_CORE + 2 * b + h, core
        )

    def image_grad(b, n):
        rows = pl.ds(b * R, n * R)

        @alone
        def _():
            for k in range(2):
                sw[pl.ds(k * H, n * R), :] = jnp.dot(
                    cf[rows, :], tu[:, pl.ds(k * H, H)], preferred_element_type=F32
                )

        def chunk(i, _):
            r = pl.ds(pl.multiple_of(b * R + i * 64, 64), 64)
            iv = inv[r, :]
            g0 = sw[pl.ds(pl.multiple_of(i * 64, 64), 64), :]
            g1 = sw[pl.ds(pl.multiple_of(H + i * 64, 64), 64), :]
            v0, v1 = u32[r, pl.ds(0, H)] * iv, u32[r, pl.ds(H, H)] * iv
            d = jnp.sum(v0 * g0 + v1 * g1, axis=-1, keepdims=True)
            g = [((g0 - v0 * d) * iv).astype(BF16), ((g1 - v1 * d) * iv).astype(BF16)]
            for t in range(3):
                for l in range(2):
                    a0, a1 = g[l][:, t * 128 : t * 128 + 128], g[l][:, 384 + t * 128 : 512 + t * 128]
                    cols = pl.ds((2 * t + l) * 128, 128)
                    gg[r, cols] = jnp.where(c == 0, a0, a1)
                    gs[r, cols] = jnp.where(c == 0, a1, a0)
            return 0

        lax.fori_loop(0, 4 * n, chunk, 0)
        g_cp[b] = send(gs.at[rows], gg.at[pl.ds(4 * R + b * R, n * R)], G_CORE + b, core)

    unit(0)
    t_core.wait_recv()
    coefs(0, 1, 0)
    xp1.wait_recv()
    xp3 = send(ff.at[half(1, 0)], ff.at[half(3, 0)], XP3, xp)
    xm1.wait_recv()
    xm3 = send(ff.at[half(1, 1)], ff.at[half(3, 1)], XM3, xm)
    unit(1)
    coefs(1, 1, 0)
    t_y.wait_recv()
    t_fwd = send(tu.at[tother], tu.at[tother], TEXT_FWD, core)
    xp2.wait_recv()
    xm2.wait_recv()
    unit(2)
    coefs(2, 1, 0)
    t_fwd.wait_recv()
    coefs(0, 3, 1)
    image_grad(0, 3)
    xp3.wait_recv()
    xm3.wait_recv()
    unit(3)
    coefs(3, 1, 0)
    coefs(3, 1, 1)
    image_grad(3, 1)
    for b in range(4):
        ft_cp[b].wait_recv()
    g_cp[0].wait_recv()
    g_cp[3].wait_recv()

    def weight(n):
        cols = pl.ds(n * 256, 256)

        @alone
        def _():
            sw[:, cols] = jnp.dot(ft[...], gg[:, cols], preferred_element_type=F32)

    def own(n, zz, k):
        return sw[pl.ds(pl.multiple_of(k * H + zz * OUT, 32), OUT), pl.ds(n * 256, 256)]

    ring = {}

    def step(n, s):
        cps = []
        for d in range(2):
            zz = (z + (4 - s if d == 0 else NZ - 4 + s)) % NZ
            i = (n * 2 + d) * 4 + s
            if s:
                ring[n, s - 1][d].wait_recv()
            for k in range(2):
                if s == 0 and k != d:
                    continue
                v = own(n, zz, k)
                if s > 1 or (s == 1 and k == d):
                    v = v + decode(zr[i - 1, pl.ds(k * OUT, OUT), :], W_CODE)
                zs[i, pl.ds(k * OUT, OUT), :] = encode(v, W_CODE)
            r = pl.ds(d * OUT, OUT) if s == 0 else pl.ds(0, 2 * OUT)
            cps.append(send(zs.at[i, r], zr.at[i, r], Z_RING + i, zp if d == 0 else zm))
        ring[n, s] = cps

    y_cp = {}

    def final(n):
        for d in range(2):
            ring[n, 3][d].wait_recv()
        cols = pl.ds(n * 256, 256)
        for k in range(2):
            r = pl.ds(k * OUT, OUT)
            v = own(n, z, k)
            for d in range(2):
                v = v + decode(zr[(n * 2 + d) * 4 + 3, r, :], W_CODE)
            zfin[r, cols] = v
            zenc[r, cols] = encode(v, W_CODE)
        for k in range(3):
            r, cc = yslice(n, (y + k + 1) % NY)
            y_cp[n, k] = send(zenc.at[r, cc], yr2.at[n, k], Y_SUM + 3 * n + k, ys[k])

    def yslice(n, yy):
        return (
            pl.ds(pl.multiple_of((yy // 2) * OUT, 32), OUT),
            pl.ds(pl.multiple_of(n * 256 + (yy % 2) * 128, 128), 128),
        )

    x_cp = []

    def over_x(n):
        r, cc = yslice(n, y)
        v = zfin[r, cc]
        for k in range(3):
            y_cp[n, k].wait_recv()
            v = v + decode(yr2[n, k], W_CODE)
        xenc[n] = encode(v, W_CODE)
        for k in range(4):
            j = n - k // 2
            if j not in (0, 1):
                continue
            xx, kc = xto[k]
            cols = pl.ds(j * 128, 128)
            cp = pltpu.make_async_remote_copy(
                xenc.at[n], xr3.at[x, :, cols], ss.at[X_SUM + len(x_cp)], rs.at[X_SUM + 4 * j + x],
                device_id=dev(xx, y, z, kc), device_id_type=MESH,
            )
            mine = (xx == x) & (kc == c)

            @pl.when(jnp.logical_not(mine))
            def _():
                cp.start()

            @pl.when(mine)
            def _():
                xr3[x, :, cols] = xenc[n]

            x_cp.append((cp, mine))

    out_cp = []

    def text_side(h, k):
        cols = pl.ds(k * H, H)

        @alone
        def _():
            pp[h, :, cols] = jnp.dot(pc[h], uu[:, cols], preferred_element_type=F32)

    p_cp = []

    def text_send():
        for i in range(4):
            r = pl.ds(i * 64, 64)
            yenc[r, :] = encode(pp[1, r, :], P_CODE)
            p_cp.append(send(yenc.at[r], yrecv.at[r], P_Y + i, yp))

    def text_out(i):
        p_cp[i].wait_recv()
        r = pl.ds(i * 64, 64)

        @alone
        def _():
            t = txr[r, :].astype(F32)
            ti = lax.rsqrt(jnp.sum(t * t, axis=-1, keepdims=True) + 1e-06)
            t = t * ti
            g = pp[0, r, :] + decode(yrecv[r, :], P_CODE)
            pp[0, r, :] = (g - t * jnp.sum(t * g, axis=-1, keepdims=True)) * ti

        cp = pltpu.make_async_copy(pp.at[0, r], tgrad_hbm.at[r], load.at[3 + i])
        cp.start()
        out_cp.append(cp)

    weight(0)
    step(0, 0)
    weight(1)
    step(1, 0)
    weight(2)
    step(2, 0)
    for b in range(4):
        u_cp[b].wait_recv()
    for key in ct_cp:
        ct_cp[key].wait_recv()
    step(0, 1)
    text_side(1, 0)
    step(1, 1)
    text_side(1, 1)
    text_send()
    step(2, 1)
    step(0, 2)
    text_side(0, 0)
    text_side(0, 1)
    step(1, 2)
    step(2, 2)
    text_out(0)
    step(0, 3)
    step(1, 3)
    text_out(1)
    step(2, 3)
    text_out(2)
    final(0)
    final(1)
    over_x(0)
    final(2)
    text_out(3)
    over_x(1)
    over_x(2)

    for j in range(2):
        for k in range(4):
            @pl.when(jnp.logical_not((k == x) & (c == xfrom)))
            def _():
                pltpu.make_async_remote_copy(
                    xenc.at[0], xr3.at[k, :, pl.ds(j * 128, 128)],
                    ss.at[X_SUM + 4 * j + k], rs.at[X_SUM + 4 * j + k],
                    device_id=core, device_id_type=MESH,
                ).wait_recv()

    v = decode(xr3[0], W_CODE)
    for k in range(1, 4):
        v = v + decode(xr3[k], W_CODE)
    mine = 2 * (x % 2) + c
    out = v[:, :OUT]
    for k, off in ((1, 96), (2, 64), (3, 160)):
        out = jnp.where(mine == k, pltpu.roll(v, 256 - off, 1)[:, :OUT], out)
    wgrad_ref[...] = out

    for cp in sent:
        cp.wait_send()
    for cp, mine in x_cp:
        @pl.when(jnp.logical_not(mine))
        def _():
            cp.wait_send()
    for cp in out_cp:
        cp.wait()


def local(feats, head_weight, text_raw, log_temp, bias):
    rows = feats.shape[0]
    factor = loss_scale / (lax.axis_size("dp") * rows * lax.axis_size("blk"))
    vmem = pltpu.VMEM
    scratch = [
        vmem((F, E), BF16),
        vmem((4 * R, F), BF16),
        vmem((F, 8 * R), BF16),
        vmem((4 * R, E), F32),
        vmem((4 * R, 1), F32),
        vmem((8 * R, E), BF16),
        vmem((R, E), BF16),
        vmem((4 * R, E), BF16),
        vmem((F, H), F32),
        vmem((2, R, 8 * R), BF16),
        vmem((2, R, 4 * R), BF16),
        vmem((4 * R, 4 * R), BF16),
        vmem((2, R, E), F32),
        vmem((R, E), BF16),
        vmem((R, E), BF16),
        vmem((8 * R, H), BF16),
        vmem((4 * R, H), BF16),
        vmem((24, 2 * OUT, 256), BF16),
        vmem((24, 2 * OUT, 256), BF16),
        vmem((2 * OUT, H), F32),
        vmem((2 * OUT, H), BF16),
        vmem((3, 3, OUT, 128), BF16),
        vmem((3, OUT, 128), BF16),
        vmem((4, OUT, 256), BF16),
        vmem((8, 128), F32),
        pltpu.SemaphoreType.DMA((7,)),
        pltpu.SemaphoreType.DMA((N_SEM,)),
        pltpu.SemaphoreType.DMA((N_SEM,)),
    ]
    anyspec = pl.BlockSpec(memory_space=pl.ANY)
    smem = pl.BlockSpec(memory_space=pltpu.SMEM)
    text_grad, weight_grad = pl.pallas_call(
        functools.partial(kernel, factor),
        out_shape=(
            jax.ShapeDtypeStruct((R, E), F32),
            jax.ShapeDtypeStruct((OUT, OUT), F32),
        ),
        in_specs=[smem, smem, anyspec, anyspec, anyspec],
        out_specs=(anyspec, pl.BlockSpec(memory_space=pltpu.VMEM)),
        scratch_shapes=scratch,
        compiler_params=pltpu.CompilerParams(
            collective_id=0, has_side_effects=True, vmem_limit_bytes=63 * 1024 * 1024
        ),
        cost_estimate=pl.CostEstimate(
            flops=20_000_000_000, bytes_accessed=8_000_000, transcendentals=4_000_000
        ),
    )(log_temp, bias, feats, head_weight, text_raw)
    scale = jnp.exp(log_temp[0])
    return scale * text_grad, scale * weight_grad


def solution(mesh):
    return jax.shard_map(
        local,
        mesh=mesh,
        in_specs=(P(("dp", "blk"), None), P(), P(("dp", "blk"), None), P(), P()),
        out_specs=(P(("dp", "blk"), None), P("dp", "blk")),
        check_vma=False,
    )
```

```python
import functools
import math

import jax
import jax.numpy as jnp
from jax import lax
from jax.experimental import pallas as pl
from jax.experimental.pallas import tpu as pltpu
from jax.sharding import PartitionSpec as P

MESH = pl.DeviceIdType.MESH
F32 = jnp.float32
BF16 = jnp.bfloat16
loss_scale = 4096.0

R = 256
E = 1536
F = 1536
H = 768
NX, NY, NZ = 4, 4, 8
OUT = 96

TEXT_CORE, TEXT_Y, TEXT_FWD = 0, 1, 2
XP1, XM1, XP2, XM2, XP3, XM3 = 3, 4, 5, 6, 7, 8
FT_CORE = 9
U_CORE = 13
CT_CORE = 17
G_CORE = 25
P_Y = 29
Z_RING = 33
Y_SUM = 81
X_SUM = 90
N_SEM = 98

P_CODE = 2.0**33
W_CODE = 2.0**4


def encode(v, s):
    v = v * s
    return (v * v * v).astype(BF16)


def decode(e, s):
    e = e.astype(F32)
    r = jnp.exp2(jnp.log2(jnp.maximum(jnp.abs(e), 1e-37)) * (1.0 / 3.0)) * (1.0 / s)
    return jnp.where(e > 0, r, jnp.where(e < 0, -r, 0.0))


def kernel(
    factor,
    lt_ref, bias_ref, feats_hbm, hw_hbm, text_hbm,
    tgrad_ref, wgrad_ref,
    hw, ff, ft, u32, inv, uu, txr, tu, sw, pc, cs, cf, pp, yenc, yrecv,
    gg, gs, zs, zr, zfin, zenc, yr2, xenc, xr3, scale_ref,
    load, ss, rs,
):
    dp, blk = lax.axis_index("dp"), lax.axis_index("blk")
    yh, z = dp // NZ, dp % NZ
    yl, x, c = blk // 8, (blk // 2) % NX, blk % 2
    y = yh * 2 + yl

    def dev(x, y, z, c):
        return ((y // 2) * NZ + z, (y % 2) * 8 + x * 2 + c)

    core = dev(x, y, z, 1 - c)
    xp, xm = dev((x + 1) % NX, y, z, c), dev((x + NX - 1) % NX, y, z, c)
    yp = dev(x, yh * 2 + 1 - yl, z, c)
    zp, zm = dev(x, y, (z + 1) % NZ, c), dev(x, y, (z + NZ - 1) % NZ, c)
    ys = [dev(x, (y + k) % NY, z, c) for k in (1, 2, 3)]
    xto = [(2 * c + k // 2, k % 2) for k in range(4)]
    xfrom = x // 2

    loads = [
        pltpu.make_async_copy(text_hbm, txr, load.at[0]),
        pltpu.make_async_copy(feats_hbm, ff.at[pl.ds(0, R)], load.at[1]),
        pltpu.make_async_copy(hw_hbm, hw, load.at[2]),
    ]
    for l in loads:
        l.start()
    bar = pltpu.get_barrier_semaphore()
    for d in [core, xp, xm, zp, zm] + ys:
        pl.semaphore_signal(bar, inc=1, device_id=d, device_id_type=MESH)
    for k in range(NX):
        @pl.when(jnp.logical_not((k == x) & (c == xfrom)))
        def _():
            pl.semaphore_signal(bar, inc=1, device_id=dev(k, y, z, xfrom), device_id_type=MESH)

    scale_ref[...] = jnp.exp(jnp.full((8, 128), lt_ref[0], F32))

    def scale():
        return scale_ref[0:1, 0:1]

    shift = bias_ref[0]

    def norm_text(i, _):
        rows = pl.ds(pl.multiple_of(i * 64, 64), 64)
        t = txr[rows, :].astype(F32)
        ti = lax.rsqrt(jnp.sum(t * t, axis=-1, keepdims=True) + 1e-06)
        tu[pl.ds(pl.multiple_of(c * R + i * 64, 64), 64), :] = (t * ti).astype(BF16)
        return 0

    pl.semaphore_wait(bar, 8 + 4 - jnp.where(c == xfrom, 1, 0))

    sent = []

    def send(src, dst, i, d, j=None):
        cp = pltpu.make_async_remote_copy(
            src, dst, ss.at[i], rs.at[i if j is None else j], device_id=d, device_id_type=MESH
        )
        cp.start()
        sent.append(cp)
        return cp

    trow = pl.ds(pl.multiple_of(c * R, R), R)
    tother = pl.ds(pl.multiple_of(2 * R + c * R, R), R)
    loads[1].wait()
    lo, hi = pl.ds(0, 128), pl.ds(128, 128)

    def half(b, k):
        return pl.ds(b * R + k * 128, 128)

    xp1 = send(ff.at[lo], ff.at[half(1, 0)], XP1, xp)
    xm1 = send(ff.at[hi], ff.at[half(1, 1)], XM1, xm)
    xp2 = send(ff.at[hi], ff.at[half(2, 0)], XP2, xp)
    xm2 = send(ff.at[lo], ff.at[half(2, 1)], XM2, xm)
    loads[0].wait()
    lax.fori_loop(0, R // 64, norm_text, 0)
    t_y = send(tu.at[trow], tu.at[tother], TEXT_Y, yp)
    t_core = send(tu.at[trow], tu.at[trow], TEXT_CORE, core)
    loads[2].wait()

    ft_cp, u_cp, ct_cp, g_cp = {}, {}, {}, {}

    alone = pl.when(dp >= 0)

    def unit(b):
        rows = pl.ds(b * R, R)

        @alone
        def _():
            u32[rows, :] = jnp.dot(ff[rows, :], hw[...], preferred_element_type=F32)
            ft[:, rows] = ff[rows, :].T

        def norm(i, _):
            r = pl.ds(pl.multiple_of(b * R + i * 64, 64), 64)
            v = u32[r, :]
            iv = lax.rsqrt(jnp.sum(v * v, axis=-1, keepdims=True) + 1e-06)
            inv[r, :] = iv
            uu[r, :] = (v * iv).astype(BF16)
            return 0

        lax.fori_loop(0, 4, norm, 0)
        u_cp[b] = send(uu.at[rows], uu.at[pl.ds(4 * R + b * R, R)], U_CORE + b, core)
        ft_cp[b] = send(
            ft.at[:, rows], ft.at[:, pl.ds(4 * R + b * R, R)], FT_CORE + b, core
        )

    def coefs(b, n, h):
        rows = pl.ds(b * R, n * R)

        @alone
        def _():
            logits = lax.dot_general(
                uu[rows, :], tu[pl.ds(2 * h * R, 2 * R), :], (((1,), (1,)), ((), ())),
                preferred_element_type=F32,
            )
            p = jax.nn.sigmoid(scale() * logits + shift)
            if h == 0 and b == 0:
                i = lax.broadcasted_iota(jnp.int32, p.shape, 0)
                j = lax.broadcasted_iota(jnp.int32, p.shape, 1)
                p = p - jnp.where(i + c * R == j, 1.0, 0.0)
            p = (factor * p).astype(BF16)
            cf[rows, pl.ds(2 * h * R, 2 * R)] = p
            t0, t1 = p[:, :R].T, p[:, R:].T
            pc[h, :, rows] = jnp.where(c == 0, t0, t1)
            cs[h, :, rows] = jnp.where(c == 0, t1, t0)

        ct_cp[b, h] = send(
            cs.at[h, :, rows], pc.at[h, :, pl.ds(4 * R + b * R, n * R)], CT_CORE + 2 * b + h, core
        )

    def image_grad(b, n):
        rows = pl.ds(b * R, n * R)

        @alone
        def _():
            for k in range(2):
                sw[pl.ds(k * H, n * R), :] = jnp.dot(
                    cf[rows, :], tu[:, pl.ds(k * H, H)], preferred_element_type=F32
                )

        def chunk(i, _):
            r = pl.ds(pl.multiple_of(b * R + i * 64, 64), 64)
            iv = inv[r, :]
            g0 = sw[pl.ds(pl.multiple_of(i * 64, 64), 64), :]
            g1 = sw[pl.ds(pl.multiple_of(H + i * 64, 64), 64), :]
            v0, v1 = u32[r, pl.ds(0, H)] * iv, u32[r, pl.ds(H, H)] * iv
            d = jnp.sum(v0 * g0 + v1 * g1, axis=-1, keepdims=True)
            g = [((g0 - v0 * d) * iv).astype(BF16), ((g1 - v1 * d) * iv).astype(BF16)]
            for t in range(3):
                for l in range(2):
                    a0, a1 = g[l][:, t * 128 : t * 128 + 128], g[l][:, 384 + t * 128 : 512 + t * 128]
                    cols = pl.ds((2 * t + l) * 128, 128)
                    gg[r, cols] = jnp.where(c == 0, a0, a1)
                    gs[r, cols] = jnp.where(c == 0, a1, a0)
            return 0

        lax.fori_loop(0, 4 * n, chunk, 0)
        g_cp[b] = send(gs.at[rows], gg.at[pl.ds(4 * R + b * R, n * R)], G_CORE + b, core)

    unit(0)
    t_core.wait_recv()
    coefs(0, 1, 0)
    xp1.wait_recv()
    xp3 = send(ff.at[half(1, 0)], ff.at[half(3, 0)], XP3, xp)
    xm1.wait_recv()
    xm3 = send(ff.at[half(1, 1)], ff.at[half(3, 1)], XM3, xm)
    unit(1)
    coefs(1, 1, 0)
    t_y.wait_recv()
    t_fwd = send(tu.at[tother], tu.at[tother], TEXT_FWD, core)
    xp2.wait_recv()
    xm2.wait_recv()
    unit(2)
    coefs(2, 1, 0)
    t_fwd.wait_recv()
    coefs(0, 3, 1)
    image_grad(0, 3)
    xp3.wait_recv()
    xm3.wait_recv()
    unit(3)
    coefs(3, 1, 0)
    coefs(3, 1, 1)
    image_grad(3, 1)
    for b in range(4):
        ft_cp[b].wait_recv()
    g_cp[0].wait_recv()
    g_cp[3].wait_recv()

    def weight(n):
        cols = pl.ds(n * 256, 256)

        @alone
        def _():
            sw[:, cols] = jnp.dot(ft[...], gg[:, cols], preferred_element_type=F32)

    def own(n, zz, k):
        return sw[pl.ds(pl.multiple_of(k * H + zz * OUT, 32), OUT), pl.ds(n * 256, 256)]

    ring = {}

    def hop(n, d, k, s):
        zz = (z + (4 - s if d == 0 else NZ - 4 + s)) % NZ
        i = (n * 2 + d) * 4 + s
        r = pl.ds(k * OUT, OUT)
        v = own(n, zz, k)
        if s > (0 if k == d else 1):
            ring[n, d, k, s - 1].wait_recv()
            v = v + decode(zr[i - 1, r, :], W_CODE)
        zs[i, r, :] = encode(v, W_CODE)
        ring[n, d, k, s] = send(
            zs.at[i, r], zr.at[i, r], Z_RING + 2 * i + k, zp if d == 0 else zm
        )

    def step(n, s):
        for d in range(2):
            hop(n, d, d, s)
        if s < 3:
            for d in range(2):
                hop(n, d, 1 - d, s + 1)

    y_cp = {}

    def final(n):
        for d in range(2):
            for k in range(2):
                ring[n, d, k, 3].wait_recv()
        cols = pl.ds(n * 256, 256)
        for k in range(2):
            r = pl.ds(k * OUT, OUT)
            v = own(n, z, k)
            for d in range(2):
                v = v + decode(zr[(n * 2 + d) * 4 + 3, r, :], W_CODE)
            zfin[r, cols] = v
            zenc[r, cols] = encode(v, W_CODE)
        for k in range(3):
            r, cc = yslice(n, (y + k + 1) % NY)
            y_cp[n, k] = send(zenc.at[r, cc], yr2.at[n, k], Y_SUM + 3 * n + k, ys[k])

    def yslice(n, yy):
        return (
            pl.ds(pl.multiple_of((yy // 2) * OUT, 32), OUT),
            pl.ds(pl.multiple_of(n * 256 + (yy % 2) * 128, 128), 128),
        )

    x_cp = []

    def over_x(n):
        r, cc = yslice(n, y)
        v = zfin[r, cc]
        for k in range(3):
            y_cp[n, k].wait_recv()
            v = v + decode(yr2[n, k], W_CODE)
        xenc[n] = encode(v, W_CODE)
        for k in range(4):
            j = n - k // 2
            if j not in (0, 1):
                continue
            xx, kc = xto[k]
            cols = pl.ds(j * 128, 128)
            cp = pltpu.make_async_remote_copy(
                xenc.at[n], xr3.at[x, :, cols], ss.at[X_SUM + len(x_cp)], rs.at[X_SUM + 4 * j + x],
                device_id=dev(xx, y, z, kc), device_id_type=MESH,
            )
            mine = (xx == x) & (kc == c)

            @pl.when(jnp.logical_not(mine))
            def _():
                cp.start()

            @pl.when(mine)
            def _():
                xr3[x, :, cols] = xenc[n]

            x_cp.append((cp, mine))


    def text_side(h, k):
        cols = pl.ds(k * H, H)

        @alone
        def _():
            pp[h, :, cols] = jnp.dot(pc[h], uu[:, cols], preferred_element_type=F32)

    p_cp = []

    def text_send():
        for i in range(4):
            r = pl.ds(i * 64, 64)
            yenc[r, :] = encode(pp[1, r, :], P_CODE)
            p_cp.append(send(yenc.at[r], yrecv.at[r], P_Y + i, yp))

    def text_out(i):
        p_cp[i].wait_recv()
        r = pl.ds(i * 64, 64)

        @alone
        def _():
            t = txr[r, :].astype(F32)
            ti = lax.rsqrt(jnp.sum(t * t, axis=-1, keepdims=True) + 1e-06)
            t = t * ti
            g = pp[0, r, :] + decode(yrecv[r, :], P_CODE)
            tgrad_ref[r, :] = (g - t * jnp.sum(t * g, axis=-1, keepdims=True)) * ti

    weight(0)
    step(0, 0)
    weight(1)
    step(1, 0)
    for b in range(4):
        u_cp[b].wait_recv()
    for key in ct_cp:
        ct_cp[key].wait_recv()
    text_side(1, 0)
    text_side(1, 1)
    text_send()
    step(0, 1)
    weight(2)
    step(2, 0)
    step(1, 1)
    step(0, 2)
    step(2, 1)
    text_side(0, 0)
    step(1, 2)
    text_side(0, 1)
    step(0, 3)
    step(2, 2)
    text_out(0)
    step(1, 3)
    text_out(1)
    final(0)
    step(2, 3)
    text_out(2)
    final(1)
    over_x(0)
    text_out(3)
    final(2)
    over_x(1)
    over_x(2)

    for j in range(2):
        for k in range(4):
            @pl.when(jnp.logical_not((k == x) & (c == xfrom)))
            def _():
                pltpu.make_async_remote_copy(
                    xenc.at[0], xr3.at[k, :, pl.ds(j * 128, 128)],
                    ss.at[X_SUM + 4 * j + k], rs.at[X_SUM + 4 * j + k],
                    device_id=core, device_id_type=MESH,
                ).wait_recv()

    v = decode(xr3[0], W_CODE)
    for k in range(1, 4):
        v = v + decode(xr3[k], W_CODE)
    mine = 2 * (x % 2) + c
    out = v[:, :OUT]
    for k, off in ((1, 96), (2, 64), (3, 160)):
        out = jnp.where(mine == k, pltpu.roll(v, 256 - off, 1)[:, :OUT], out)
    wgrad_ref[...] = out

    for cp in sent:
        cp.wait_send()
    for cp, mine in x_cp:
        @pl.when(jnp.logical_not(mine))
        def _():
            cp.wait_send()


def local(feats, head_weight, text_raw, log_temp, bias):
    rows = feats.shape[0]
    factor = loss_scale / (lax.axis_size("dp") * rows * lax.axis_size("blk"))
    vmem = pltpu.VMEM
    scratch = [
        vmem((F, E), BF16),
        vmem((4 * R, F), BF16),
        vmem((F, 8 * R), BF16),
        vmem((4 * R, E), F32),
        vmem((4 * R, 1), F32),
        vmem((8 * R, E), BF16),
        vmem((R, E), BF16),
        vmem((4 * R, E), BF16),
        vmem((F, H), F32),
        vmem((2, R, 8 * R), BF16),
        vmem((2, R, 4 * R), BF16),
        vmem((4 * R, 4 * R), BF16),
        vmem((2, R, E), F32),
        vmem((R, E), BF16),
        vmem((R, E), BF16),
        vmem((8 * R, H), BF16),
        vmem((4 * R, H), BF16),
        vmem((24, 2 * OUT, 256), BF16),
        vmem((24, 2 * OUT, 256), BF16),
        vmem((2 * OUT, H), F32),
        vmem((2 * OUT, H), BF16),
        vmem((3, 3, OUT, 128), BF16),
        vmem((3, OUT, 128), BF16),
        vmem((4, OUT, 256), BF16),
        vmem((8, 128), F32),
        pltpu.SemaphoreType.DMA((3,)),
        pltpu.SemaphoreType.DMA((N_SEM,)),
        pltpu.SemaphoreType.DMA((N_SEM,)),
    ]
    anyspec = pl.BlockSpec(memory_space=pl.ANY)
    smem = pl.BlockSpec(memory_space=pltpu.SMEM)
    text_grad, weight_grad = pl.pallas_call(
        functools.partial(kernel, factor),
        out_shape=(
            pltpu.VMEM((R, E), F32),
            jax.ShapeDtypeStruct((OUT, OUT), F32),
        ),
        in_specs=[smem, smem, anyspec, anyspec, anyspec],
        out_specs=(pl.BlockSpec(memory_space=pltpu.VMEM), pl.BlockSpec(memory_space=pltpu.VMEM)),
        scratch_shapes=scratch,
        compiler_params=pltpu.CompilerParams(
            collective_id=0, has_side_effects=True, vmem_limit_bytes=59 * 1024 * 1024
        ),
        cost_estimate=pl.CostEstimate(
            flops=20_000_000_000, bytes_accessed=8_000_000, transcendentals=4_000_000
        ),
    )(log_temp, bias, feats, head_weight, text_raw)
    scale = jnp.exp(log_temp[0])
    return scale * text_grad, scale * weight_grad


def solution(mesh):
    return jax.shard_map(
        local,
        mesh=mesh,
        in_specs=(P(("dp", "blk"), None), P(), P(("dp", "blk"), None), P(), P()),
        out_specs=(P(("dp", "blk"), None), P("dp", "blk")),
        check_vma=False,
    )
```

```python
import functools
import math

import jax
import jax.numpy as jnp
from jax import lax
from jax.experimental import pallas as pl
from jax.experimental.pallas import tpu as pltpu
from jax.sharding import PartitionSpec as P

MESH = pl.DeviceIdType.MESH
F32 = jnp.float32
BF16 = jnp.bfloat16
loss_scale = 4096.0

R = 256
E = 1536
F = 1536
H = 768
NX, NY, NZ = 4, 4, 8
OUT = 96

TEXT_CORE, TEXT_Y, TEXT_FWD = 0, 1, 2
XP1, XM1, XP2, XM2, XP3, XM3 = 3, 4, 5, 6, 7, 8
FT_CORE = 9
U_CORE = 13
CT_CORE = 17
G_CORE = 25
P_Y = 29
Z_RING = 33
Y_SUM = 81
X_SUM = 90
N_SEM = 98

P_CODE = 2.0**33
W_CODE = 2.0**4


def encode(v, s):
    v = v * s
    return (v * v * v).astype(BF16)


def decode(e, s):
    e = e.astype(F32)
    r = jnp.exp2(jnp.log2(jnp.maximum(jnp.abs(e), 1e-37)) * (1.0 / 3.0)) * (1.0 / s)
    return jnp.where(e > 0, r, jnp.where(e < 0, -r, 0.0))


def kernel(
    factor,
    lt_ref, bias_ref, feats_hbm, hw_hbm, text_hbm,
    tgrad_ref, wgrad_ref,
    hw, ff, ft, u32, inv, uu, txr, tu, sw, pc, cs, cf, pp, yenc, yrecv,
    gg, gs, zs, zr, zfin, zenc, yr2, xenc, xr3, scale_ref,
    load, ss, rs,
):
    dp, blk = lax.axis_index("dp"), lax.axis_index("blk")
    yh, z = dp // NZ, dp % NZ
    yl, x, c = blk // 8, (blk // 2) % NX, blk % 2
    y = yh * 2 + yl

    def dev(x, y, z, c):
        return ((y // 2) * NZ + z, (y % 2) * 8 + x * 2 + c)

    core = dev(x, y, z, 1 - c)
    xp, xm = dev((x + 1) % NX, y, z, c), dev((x + NX - 1) % NX, y, z, c)
    yp = dev(x, yh * 2 + 1 - yl, z, c)
    zp, zm = dev(x, y, (z + 1) % NZ, c), dev(x, y, (z + NZ - 1) % NZ, c)
    ys = [dev(x, (y + k) % NY, z, c) for k in (1, 2, 3)]
    xto = [(2 * c + k // 2, k % 2) for k in range(4)]
    xfrom = x // 2

    loads = [
        pltpu.make_async_copy(text_hbm, txr, load.at[0]),
        pltpu.make_async_copy(feats_hbm, ff.at[pl.ds(0, R)], load.at[1]),
        pltpu.make_async_copy(hw_hbm, hw, load.at[2]),
    ]
    for l in loads:
        l.start()
    bar = pltpu.get_barrier_semaphore()
    for d in [core, xp, xm, zp, zm] + ys:
        pl.semaphore_signal(bar, inc=1, device_id=d, device_id_type=MESH)
    for k in range(NX):
        @pl.when(jnp.logical_not((k == x) & (c == xfrom)))
        def _():
            pl.semaphore_signal(bar, inc=1, device_id=dev(k, y, z, xfrom), device_id_type=MESH)

    scale_ref[...] = jnp.exp(jnp.full((8, 128), lt_ref[0], F32))

    def scale():
        return scale_ref[0:1, 0:1]

    shift = bias_ref[0]

    def norm_text(i, _):
        rows = pl.ds(pl.multiple_of(i * 64, 64), 64)
        t = txr[rows, :].astype(F32)
        ti = lax.rsqrt(jnp.sum(t * t, axis=-1, keepdims=True) + 1e-06)
        tu[pl.ds(pl.multiple_of(c * R + i * 64, 64), 64), :] = (t * ti).astype(BF16)
        return 0

    pl.semaphore_wait(bar, 8 + 4 - jnp.where(c == xfrom, 1, 0))

    sent = []

    def send(src, dst, i, d, j=None):
        cp = pltpu.make_async_remote_copy(
            src, dst, ss.at[i], rs.at[i if j is None else j], device_id=d, device_id_type=MESH
        )
        cp.start()
        sent.append(cp)
        return cp

    trow = pl.ds(pl.multiple_of(c * R, R), R)
    tother = pl.ds(pl.multiple_of(2 * R + c * R, R), R)
    loads[1].wait()
    lo, hi = pl.ds(0, 128), pl.ds(128, 128)

    def half(b, k):
        return pl.ds(b * R + k * 128, 128)

    xp1 = send(ff.at[lo], ff.at[half(1, 0)], XP1, xp)
    xm1 = send(ff.at[hi], ff.at[half(1, 1)], XM1, xm)
    xp2 = send(ff.at[hi], ff.at[half(2, 0)], XP2, xp)
    xm2 = send(ff.at[lo], ff.at[half(2, 1)], XM2, xm)
    loads[0].wait()
    lax.fori_loop(0, R // 64, norm_text, 0)
    t_y = send(tu.at[trow], tu.at[tother], TEXT_Y, yp)
    t_core = send(tu.at[trow], tu.at[trow], TEXT_CORE, core)
    loads[2].wait()

    ft_cp, u_cp, ct_cp, g_cp = {}, {}, {}, {}

    alone = pl.when(dp >= 0)

    def unit(b):
        rows = pl.ds(b * R, R)

        @alone
        def _():
            u32[rows, :] = jnp.dot(ff[rows, :], hw[...], preferred_element_type=F32)
            ft[:, rows] = ff[rows, :].T

        def norm(i, _):
            r = pl.ds(pl.multiple_of(b * R + i * 64, 64), 64)
            v = u32[r, :]
            iv = lax.rsqrt(jnp.sum(v * v, axis=-1, keepdims=True) + 1e-06)
            inv[r, :] = iv
            uu[r, :] = (v * iv).astype(BF16)
            return 0

        lax.fori_loop(0, 4, norm, 0)
        u_cp[b] = send(uu.at[rows], uu.at[pl.ds(4 * R + b * R, R)], U_CORE + b, core)
        ft_cp[b] = send(
            ft.at[:, rows], ft.at[:, pl.ds(4 * R + b * R, R)], FT_CORE + b, core
        )

    def coefs(b, n, h):
        rows = pl.ds(b * R, n * R)

        @alone
        def _():
            logits = lax.dot_general(
                uu[rows, :], tu[pl.ds(2 * h * R, 2 * R), :], (((1,), (1,)), ((), ())),
                preferred_element_type=F32,
            )
            p = jax.nn.sigmoid(scale() * logits + shift)
            if h == 0 and b == 0:
                i = lax.broadcasted_iota(jnp.int32, p.shape, 0)
                j = lax.broadcasted_iota(jnp.int32, p.shape, 1)
                p = p - jnp.where(i + c * R == j, 1.0, 0.0)
            p = (factor * p).astype(BF16)
            cf[rows, pl.ds(2 * h * R, 2 * R)] = p
            t0, t1 = p[:, :R].T, p[:, R:].T
            pc[h, :, rows] = jnp.where(c == 0, t0, t1)
            cs[h, :, rows] = jnp.where(c == 0, t1, t0)

        ct_cp[b, h] = send(
            cs.at[h, :, rows], pc.at[h, :, pl.ds(4 * R + b * R, n * R)], CT_CORE + 2 * b + h, core
        )

    def image_grad(b, n):
        rows = pl.ds(b * R, n * R)

        @alone
        def _():
            for k in range(2):
                sw[pl.ds(k * H, n * R), :] = jnp.dot(
                    cf[rows, :], tu[:, pl.ds(k * H, H)], preferred_element_type=F32
                )

        def chunk(i, _):
            r = pl.ds(pl.multiple_of(b * R + i * 64, 64), 64)
            iv = inv[r, :]
            g0 = sw[pl.ds(pl.multiple_of(i * 64, 64), 64), :]
            g1 = sw[pl.ds(pl.multiple_of(H + i * 64, 64), 64), :]
            v0, v1 = u32[r, pl.ds(0, H)] * iv, u32[r, pl.ds(H, H)] * iv
            d = jnp.sum(v0 * g0 + v1 * g1, axis=-1, keepdims=True)
            g = [((g0 - v0 * d) * iv).astype(BF16), ((g1 - v1 * d) * iv).astype(BF16)]
            for t in range(3):
                for l in range(2):
                    a0, a1 = g[l][:, t * 128 : t * 128 + 128], g[l][:, 384 + t * 128 : 512 + t * 128]
                    cols = pl.ds((2 * t + l) * 128, 128)
                    gg[r, cols] = jnp.where(c == 0, a0, a1)
                    gs[r, cols] = jnp.where(c == 0, a1, a0)
            return 0

        lax.fori_loop(0, 4 * n, chunk, 0)
        g_cp[b] = send(gs.at[rows], gg.at[pl.ds(4 * R + b * R, n * R)], G_CORE + b, core)

    unit(0)
    t_core.wait_recv()
    coefs(0, 1, 0)
    xp1.wait_recv()
    xp3 = send(ff.at[half(1, 0)], ff.at[half(3, 0)], XP3, xp)
    xm1.wait_recv()
    xm3 = send(ff.at[half(1, 1)], ff.at[half(3, 1)], XM3, xm)
    unit(1)
    coefs(1, 1, 0)
    t_y.wait_recv()
    t_fwd = send(tu.at[tother], tu.at[tother], TEXT_FWD, core)
    xp2.wait_recv()
    xm2.wait_recv()
    unit(2)
    coefs(2, 1, 0)
    t_fwd.wait_recv()
    coefs(0, 3, 1)
    image_grad(0, 3)
    xp3.wait_recv()
    xm3.wait_recv()
    unit(3)
    coefs(3, 1, 0)
    coefs(3, 1, 1)
    image_grad(3, 1)
    for b in range(4):
        ft_cp[b].wait_recv()
    g_cp[0].wait_recv()
    g_cp[3].wait_recv()

    def weight(n):
        cols = pl.ds(n * 256, 256)

        @alone
        def _():
            sw[:, cols] = jnp.dot(ft[...], gg[:, cols], preferred_element_type=F32)

    def own(n, zz, k):
        return sw[pl.ds(pl.multiple_of(k * H + zz * OUT, 32), OUT), pl.ds(n * 256, 256)]

    ring = {}

    def hop(n, d, k, s):
        zz = (z + (4 - s if d == 0 else NZ - 4 + s)) % NZ
        i = (n * 2 + d) * 4 + s
        r = pl.ds(k * OUT, OUT)
        v = own(n, zz, k)
        if s > (0 if k == d else 1):
            ring[n, d, k, s - 1].wait_recv()
            v = v + decode(zr[i - 1, r, :], W_CODE)
        zs[i, r, :] = encode(v, W_CODE)
        ring[n, d, k, s] = send(
            zs.at[i, r], zr.at[i, r], Z_RING + 2 * i + k, zp if d == 0 else zm
        )

    def step(n, s):
        for d in range(2):
            hop(n, d, d, s)
        if s < 3:
            for d in range(2):
                hop(n, d, 1 - d, s + 1)

    y_cp = {}

    def final(n):
        for d in range(2):
            for k in range(2):
                ring[n, d, k, 3].wait_recv()
        cols = pl.ds(n * 256, 256)
        for k in range(2):
            r = pl.ds(k * OUT, OUT)
            v = own(n, z, k)
            for d in range(2):
                v = v + decode(zr[(n * 2 + d) * 4 + 3, r, :], W_CODE)
            zfin[r, cols] = v
            zenc[r, cols] = encode(v, W_CODE)
        for k in range(3):
            r, cc = yslice(n, (y + k + 1) % NY)
            y_cp[n, k] = send(zenc.at[r, cc], yr2.at[n, k], Y_SUM + 3 * n + k, ys[k])

    def yslice(n, yy):
        return (
            pl.ds(pl.multiple_of((yy // 2) * OUT, 32), OUT),
            pl.ds(pl.multiple_of(n * 256 + (yy % 2) * 128, 128), 128),
        )

    x_cp = []

    def over_x(n):
        r, cc = yslice(n, y)
        v = zfin[r, cc]
        for k in range(3):
            y_cp[n, k].wait_recv()
            v = v + decode(yr2[n, k], W_CODE)
        xenc[n] = encode(v, W_CODE)
        for k in range(4):
            j = n - k // 2
            if j not in (0, 1):
                continue
            xx, kc = xto[k]
            cols = pl.ds(j * 128, 128)
            cp = pltpu.make_async_remote_copy(
                xenc.at[n], xr3.at[x, :, cols], ss.at[X_SUM + len(x_cp)], rs.at[X_SUM + 4 * j + x],
                device_id=dev(xx, y, z, kc), device_id_type=MESH,
            )
            mine = (xx == x) & (kc == c)

            @pl.when(jnp.logical_not(mine))
            def _():
                cp.start()

            @pl.when(mine)
            def _():
                xr3[x, :, cols] = xenc[n]

            x_cp.append((cp, mine))


    def text_side(h, k):
        cols = pl.ds(k * H, H)

        @alone
        def _():
            pp[h, :, cols] = jnp.dot(pc[h], uu[:, cols], preferred_element_type=F32)

    p_cp = []

    def text_send():
        for i in range(4):
            r = pl.ds(i * 64, 64)
            yenc[r, :] = encode(pp[1, r, :], P_CODE)
            p_cp.append(send(yenc.at[r], yrecv.at[r], P_Y + i, yp))

    def text_out(i):
        p_cp[i].wait_recv()
        r = pl.ds(i * 64, 64)

        @alone
        def _():
            t = txr[r, :].astype(F32)
            ti = lax.rsqrt(jnp.sum(t * t, axis=-1, keepdims=True) + 1e-06)
            t = t * ti
            g = pp[0, r, :] + decode(yrecv[r, :], P_CODE)
            tgrad_ref[r, :] = (g - t * jnp.sum(t * g, axis=-1, keepdims=True)) * ti

    weight(0)
    step(0, 0)
    weight(1)
    step(1, 0)
    for b in range(4):
        u_cp[b].wait_recv()
    for key in ct_cp:
        ct_cp[key].wait_recv()
    text_side(1, 0)
    text_side(1, 1)
    text_send()
    step(0, 1)
    weight(2)
    step(2, 0)
    step(1, 1)
    step(0, 2)
    step(2, 1)
    text_side(0, 0)
    step(1, 2)
    text_side(0, 1)
    step(0, 3)
    step(2, 2)
    text_out(0)
    step(1, 3)
    final(0)
    text_out(1)
    step(2, 3)
    final(1)
    over_x(0)
    final(2)
    text_out(2)
    over_x(1)
    text_out(3)
    over_x(2)

    for j in range(2):
        for k in range(4):
            @pl.when(jnp.logical_not((k == x) & (c == xfrom)))
            def _():
                pltpu.make_async_remote_copy(
                    xenc.at[0], xr3.at[k, :, pl.ds(j * 128, 128)],
                    ss.at[X_SUM + 4 * j + k], rs.at[X_SUM + 4 * j + k],
                    device_id=core, device_id_type=MESH,
                ).wait_recv()

    v = decode(xr3[0], W_CODE)
    for k in range(1, 4):
        v = v + decode(xr3[k], W_CODE)
    mine = 2 * (x % 2) + c
    out = v[:, :OUT]
    for k, off in ((1, 96), (2, 64), (3, 160)):
        out = jnp.where(mine == k, pltpu.roll(v, 256 - off, 1)[:, :OUT], out)
    wgrad_ref[...] = out

    for cp in sent:
        cp.wait_send()
    for cp, mine in x_cp:
        @pl.when(jnp.logical_not(mine))
        def _():
            cp.wait_send()


def local(feats, head_weight, text_raw, log_temp, bias):
    rows = feats.shape[0]
    factor = loss_scale / (lax.axis_size("dp") * rows * lax.axis_size("blk"))
    vmem = pltpu.VMEM
    scratch = [
        vmem((F, E), BF16),
        vmem((4 * R, F), BF16),
        vmem((F, 8 * R), BF16),
        vmem((4 * R, E), F32),
        vmem((4 * R, 1), F32),
        vmem((8 * R, E), BF16),
        vmem((R, E), BF16),
        vmem((4 * R, E), BF16),
        vmem((F, H), F32),
        vmem((2, R, 8 * R), BF16),
        vmem((2, R, 4 * R), BF16),
        vmem((4 * R, 4 * R), BF16),
        vmem((2, R, E), F32),
        vmem((R, E), BF16),
        vmem((R, E), BF16),
        vmem((8 * R, H), BF16),
        vmem((4 * R, H), BF16),
        vmem((24, 2 * OUT, 256), BF16),
        vmem((24, 2 * OUT, 256), BF16),
        vmem((2 * OUT, H), F32),
        vmem((2 * OUT, H), BF16),
        vmem((3, 3, OUT, 128), BF16),
        vmem((3, OUT, 128), BF16),
        vmem((4, OUT, 256), BF16),
        vmem((8, 128), F32),
        pltpu.SemaphoreType.DMA((3,)),
        pltpu.SemaphoreType.DMA((N_SEM,)),
        pltpu.SemaphoreType.DMA((N_SEM,)),
    ]
    anyspec = pl.BlockSpec(memory_space=pl.ANY)
    smem = pl.BlockSpec(memory_space=pltpu.SMEM)
    text_grad, weight_grad = pl.pallas_call(
        functools.partial(kernel, factor),
        out_shape=(
            pltpu.VMEM((R, E), F32),
            jax.ShapeDtypeStruct((OUT, OUT), F32),
        ),
        in_specs=[smem, smem, anyspec, anyspec, anyspec],
        out_specs=(pl.BlockSpec(memory_space=pltpu.VMEM), pl.BlockSpec(memory_space=pltpu.VMEM)),
        scratch_shapes=scratch,
        compiler_params=pltpu.CompilerParams(
            collective_id=0, has_side_effects=True, vmem_limit_bytes=59 * 1024 * 1024
        ),
        cost_estimate=pl.CostEstimate(
            flops=20_000_000_000, bytes_accessed=8_000_000, transcendentals=4_000_000
        ),
    )(log_temp, bias, feats, head_weight, text_raw)
    scale = jnp.exp(log_temp[0])
    return scale * text_grad, scale * weight_grad


def solution(mesh):
    return jax.shard_map(
        local,
        mesh=mesh,
        in_specs=(P(("dp", "blk"), None), P(), P(("dp", "blk"), None), P(), P()),
        out_specs=(P(("dp", "blk"), None), P("dp", "blk")),
        check_vma=False,
    )
```

```python
import functools
import math

import jax
import jax.numpy as jnp
from jax import lax
from jax.experimental import pallas as pl
from jax.experimental.pallas import tpu as pltpu
from jax.sharding import PartitionSpec as P

MESH = pl.DeviceIdType.MESH
F32 = jnp.float32
BF16 = jnp.bfloat16
loss_scale = 4096.0

R = 256
E = 1536
F = 1536
H = 768
NX, NY, NZ = 4, 4, 8
OUT = 96

TEXT_CORE, TEXT_Y, TEXT_FWD = 0, 1, 2
XP1, XM1, XP2, XM2, XP3, XM3 = 3, 4, 5, 6, 7, 8
FT_CORE = 9
U_CORE = 13
CT_CORE = 17
G_CORE = 25
P_Y = 29
Z_RING = 33
Y_SUM = 81
X_SUM = 90
N_SEM = 98

P_CODE = 2.0**33
W_CODE = 2.0**4


def encode(v, s):
    v = v * s
    return (v * v * v).astype(BF16)


def decode(e, s):
    e = e.astype(F32)
    r = jnp.exp2(jnp.log2(jnp.maximum(jnp.abs(e), 1e-37)) * (1.0 / 3.0)) * (1.0 / s)
    return jnp.where(e > 0, r, jnp.where(e < 0, -r, 0.0))


def kernel(
    factor,
    lt_ref, bias_ref, feats_hbm, hw_hbm, text_hbm,
    tgrad_ref, wgrad_ref,
    hw, ff, ft, u32, inv, uu, txr, tu, sw, pc, cs, cf, pp, yenc, yrecv,
    gg, gs, zs, zr, zfin, zenc, yr2, xenc, xr3, scale_ref,
    load, ss, rs,
):
    dp, blk = lax.axis_index("dp"), lax.axis_index("blk")
    yh, z = dp // NZ, dp % NZ
    yl, x, c = blk // 8, (blk // 2) % NX, blk % 2
    y = yh * 2 + yl

    def dev(x, y, z, c):
        return ((y // 2) * NZ + z, (y % 2) * 8 + x * 2 + c)

    core = dev(x, y, z, 1 - c)
    xp, xm = dev((x + 1) % NX, y, z, c), dev((x + NX - 1) % NX, y, z, c)
    yp = dev(x, yh * 2 + 1 - yl, z, c)
    zp, zm = dev(x, y, (z + 1) % NZ, c), dev(x, y, (z + NZ - 1) % NZ, c)
    ys = [dev(x, (y + k) % NY, z, c) for k in (1, 2, 3)]
    xto = [(2 * c + k // 2, k % 2) for k in range(4)]
    xfrom = x // 2

    loads = [
        pltpu.make_async_copy(text_hbm, txr, load.at[0]),
        pltpu.make_async_copy(feats_hbm, ff.at[pl.ds(0, R)], load.at[1]),
        pltpu.make_async_copy(hw_hbm, hw, load.at[2]),
    ]
    for l in loads:
        l.start()
    bar = pltpu.get_barrier_semaphore()
    for d in [core, xp, xm, zp, zm] + ys:
        pl.semaphore_signal(bar, inc=1, device_id=d, device_id_type=MESH)
    for k in range(NX):
        @pl.when(jnp.logical_not((k == x) & (c == xfrom)))
        def _():
            pl.semaphore_signal(bar, inc=1, device_id=dev(k, y, z, xfrom), device_id_type=MESH)

    scale_ref[...] = jnp.exp(jnp.full((8, 128), lt_ref[0], F32))

    def scale():
        return scale_ref[0:1, 0:1]

    shift = bias_ref[0]

    def norm_text(i, _):
        rows = pl.ds(pl.multiple_of(i * 64, 64), 64)
        t = txr[rows, :].astype(F32)
        ti = lax.rsqrt(jnp.sum(t * t, axis=-1, keepdims=True) + 1e-06)
        tu[pl.ds(pl.multiple_of(c * R + i * 64, 64), 64), :] = (t * ti).astype(BF16)
        return 0

    pl.semaphore_wait(bar, 8 + 4 - jnp.where(c == xfrom, 1, 0))

    sent = []

    def send(src, dst, i, d, j=None):
        cp = pltpu.make_async_remote_copy(
            src, dst, ss.at[i], rs.at[i if j is None else j], device_id=d, device_id_type=MESH
        )
        cp.start()
        sent.append(cp)
        return cp

    trow = pl.ds(pl.multiple_of(c * R, R), R)
    tother = pl.ds(pl.multiple_of(2 * R + c * R, R), R)
    loads[1].wait()
    lo, hi = pl.ds(0, 128), pl.ds(128, 128)

    def half(b, k):
        return pl.ds(b * R + k * 128, 128)

    xp1 = send(ff.at[lo], ff.at[half(1, 0)], XP1, xp)
    xm1 = send(ff.at[hi], ff.at[half(1, 1)], XM1, xm)
    xp2 = send(ff.at[hi], ff.at[half(2, 0)], XP2, xp)
    xm2 = send(ff.at[lo], ff.at[half(2, 1)], XM2, xm)
    loads[0].wait()
    lax.fori_loop(0, R // 64, norm_text, 0)
    t_y = send(tu.at[trow], tu.at[tother], TEXT_Y, yp)
    t_core = send(tu.at[trow], tu.at[trow], TEXT_CORE, core)
    loads[2].wait()

    ft_cp, u_cp, ct_cp, g_cp = {}, {}, {}, {}

    alone = pl.when(dp >= 0)

    def unit(b):
        rows = pl.ds(b * R, R)

        @alone
        def _():
            u32[rows, :] = jnp.dot(ff[rows, :], hw[...], preferred_element_type=F32)
            ft[:, rows] = ff[rows, :].T

        def norm(i, _):
            r = pl.ds(pl.multiple_of(b * R + i * 64, 64), 64)
            v = u32[r, :]
            iv = lax.rsqrt(jnp.sum(v * v, axis=-1, keepdims=True) + 1e-06)
            inv[r, :] = iv
            uu[r, :] = (v * iv).astype(BF16)
            return 0

        lax.fori_loop(0, 4, norm, 0)
        u_cp[b] = send(uu.at[rows], uu.at[pl.ds(4 * R + b * R, R)], U_CORE + b, core)
        ft_cp[b] = send(
            ft.at[:, rows], ft.at[:, pl.ds(4 * R + b * R, R)], FT_CORE + b, core
        )

    def coefs(b, n, h):
        rows = pl.ds(b * R, n * R)

        @alone
        def _():
            logits = lax.dot_general(
                uu[rows, :], tu[pl.ds(2 * h * R, 2 * R), :], (((1,), (1,)), ((), ())),
                preferred_element_type=F32,
            )
            p = jax.nn.sigmoid(scale() * logits + shift)
            if h == 0 and b == 0:
                i = lax.broadcasted_iota(jnp.int32, p.shape, 0)
                j = lax.broadcasted_iota(jnp.int32, p.shape, 1)
                p = p - jnp.where(i + c * R == j, 1.0, 0.0)
            p = (factor * p).astype(BF16)
            cf[rows, pl.ds(2 * h * R, 2 * R)] = p
            t0, t1 = p[:, :R].T, p[:, R:].T
            pc[h, :, rows] = jnp.where(c == 0, t0, t1)
            cs[h, :, rows] = jnp.where(c == 0, t1, t0)

        ct_cp[b, h] = send(
            cs.at[h, :, rows], pc.at[h, :, pl.ds(4 * R + b * R, n * R)], CT_CORE + 2 * b + h, core
        )

    def image_grad(b, n):
        rows = pl.ds(b * R, n * R)

        @alone
        def _():
            for k in range(2):
                sw[pl.ds(k * H, n * R), :] = jnp.dot(
                    cf[rows, :], tu[:, pl.ds(k * H, H)], preferred_element_type=F32
                )

        def chunk(i, _):
            r = pl.ds(pl.multiple_of(b * R + i * 64, 64), 64)
            iv = inv[r, :]
            g0 = sw[pl.ds(pl.multiple_of(i * 64, 64), 64), :]
            g1 = sw[pl.ds(pl.multiple_of(H + i * 64, 64), 64), :]
            v0, v1 = u32[r, pl.ds(0, H)] * iv, u32[r, pl.ds(H, H)] * iv
            d = jnp.sum(v0 * g0 + v1 * g1, axis=-1, keepdims=True)
            g = [((g0 - v0 * d) * iv).astype(BF16), ((g1 - v1 * d) * iv).astype(BF16)]
            for t in range(3):
                for l in range(2):
                    a0, a1 = g[l][:, t * 128 : t * 128 + 128], g[l][:, 384 + t * 128 : 512 + t * 128]
                    cols = pl.ds((2 * t + l) * 128, 128)
                    gg[r, cols] = jnp.where(c == 0, a0, a1)
                    gs[r, cols] = jnp.where(c == 0, a1, a0)
            return 0

        lax.fori_loop(0, 4 * n, chunk, 0)
        g_cp[b] = send(gs.at[rows], gg.at[pl.ds(4 * R + b * R, n * R)], G_CORE + b, core)

    unit(0)
    t_core.wait_recv()
    coefs(0, 1, 0)
    xp1.wait_recv()
    xp3 = send(ff.at[half(1, 0)], ff.at[half(3, 0)], XP3, xp)
    xm1.wait_recv()
    xm3 = send(ff.at[half(1, 1)], ff.at[half(3, 1)], XM3, xm)
    unit(1)
    coefs(1, 1, 0)
    t_y.wait_recv()
    t_fwd = send(tu.at[tother], tu.at[tother], TEXT_FWD, core)
    xp2.wait_recv()
    xm2.wait_recv()
    unit(2)
    coefs(2, 1, 0)
    t_fwd.wait_recv()
    coefs(0, 3, 1)
    image_grad(0, 3)
    xp3.wait_recv()
    xm3.wait_recv()
    unit(3)
    coefs(3, 1, 0)
    coefs(3, 1, 1)
    image_grad(3, 1)
    for b in range(4):
        ft_cp[b].wait_recv()
    g_cp[0].wait_recv()
    g_cp[3].wait_recv()

    def weight(n):
        cols = pl.ds(n * 256, 256)

        @alone
        def _():
            sw[:, cols] = jnp.dot(ft[...], gg[:, cols], preferred_element_type=F32)

    def own(n, zz, k):
        return sw[pl.ds(pl.multiple_of(k * H + zz * OUT, 32), OUT), pl.ds(n * 256, 256)]

    ring = {}

    def hop(n, d, k, s):
        zz = (z + (4 - s if d == 0 else NZ - 4 + s)) % NZ
        i = (n * 2 + d) * 4 + s
        r = pl.ds(k * OUT, OUT)
        v = own(n, zz, k)
        if s > (0 if k == d else 1):
            ring[n, d, k, s - 1].wait_recv()
            v = v + decode(zr[i - 1, r, :], W_CODE)
        zs[i, r, :] = encode(v, W_CODE)
        ring[n, d, k, s] = send(
            zs.at[i, r], zr.at[i, r], Z_RING + 2 * i + k, zp if d == 0 else zm
        )

    def step(n, s):
        for d in range(2):
            hop(n, d, d, s)
        if s < 3:
            for d in range(2):
                hop(n, d, 1 - d, s + 1)

    y_cp = {}

    def final(n):
        for d in range(2):
            for k in range(2):
                ring[n, d, k, 3].wait_recv()
        cols = pl.ds(n * 256, 256)

        @alone
        def _():
            for k in range(2):
                r = pl.ds(k * OUT, OUT)
                v = own(n, z, k)
                for d in range(2):
                    v = v + decode(zr[(n * 2 + d) * 4 + 3, r, :], W_CODE)
                zfin[r, cols] = v
                zenc[r, cols] = encode(v, W_CODE)

        for k in range(3):
            r, cc = yslice(n, (y + k + 1) % NY)
            y_cp[n, k] = send(zenc.at[r, cc], yr2.at[n, k], Y_SUM + 3 * n + k, ys[k])

    def yslice(n, yy):
        return (
            pl.ds(pl.multiple_of((yy // 2) * OUT, 32), OUT),
            pl.ds(pl.multiple_of(n * 256 + (yy % 2) * 128, 128), 128),
        )

    x_cp = []

    def over_x(n):
        r, cc = yslice(n, y)
        v = zfin[r, cc]
        for k in range(3):
            y_cp[n, k].wait_recv()
            v = v + decode(yr2[n, k], W_CODE)
        xenc[n] = encode(v, W_CODE)
        for k in range(4):
            j = n - k // 2
            if j not in (0, 1):
                continue
            xx, kc = xto[k]
            cols = pl.ds(j * 128, 128)
            cp = pltpu.make_async_remote_copy(
                xenc.at[n], xr3.at[x, :, cols], ss.at[X_SUM + len(x_cp)], rs.at[X_SUM + 4 * j + x],
                device_id=dev(xx, y, z, kc), device_id_type=MESH,
            )
            mine = (xx == x) & (kc == c)

            @pl.when(jnp.logical_not(mine))
            def _():
                cp.start()

            @pl.when(mine)
            def _():
                xr3[x, :, cols] = xenc[n]

            x_cp.append((cp, mine))


    def text_side(h, k):
        cols = pl.ds(k * H, H)

        @alone
        def _():
            pp[h, :, cols] = jnp.dot(pc[h], uu[:, cols], preferred_element_type=F32)

    p_cp = []

    def text_send():
        for i in range(4):
            r = pl.ds(i * 64, 64)

            @alone
            def _():
                yenc[r, :] = encode(pp[1, r, :], P_CODE)

            p_cp.append(send(yenc.at[r], yrecv.at[r], P_Y + i, yp))

    def text_out(i):
        p_cp[i].wait_recv()
        r = pl.ds(i * 64, 64)

        @alone
        def _():
            t = txr[r, :].astype(F32)
            ti = lax.rsqrt(jnp.sum(t * t, axis=-1, keepdims=True) + 1e-06)
            t = t * ti
            g = pp[0, r, :] + decode(yrecv[r, :], P_CODE)
            tgrad_ref[r, :] = (g - t * jnp.sum(t * g, axis=-1, keepdims=True)) * ti

    weight(0)
    step(0, 0)
    weight(1)
    step(1, 0)
    for b in range(4):
        u_cp[b].wait_recv()
    for key in ct_cp:
        ct_cp[key].wait_recv()
    text_side(1, 0)
    text_side(1, 1)
    text_send()
    step(0, 1)
    weight(2)
    step(2, 0)
    step(1, 1)
    step(0, 2)
    step(2, 1)
    text_side(0, 0)
    step(1, 2)
    text_side(0, 1)
    step(0, 3)
    step(2, 2)
    text_out(0)
    step(1, 3)
    text_out(1)
    final(0)
    step(2, 3)
    text_out(2)
    final(1)
    over_x(0)
    text_out(3)
    final(2)
    over_x(1)
    over_x(2)

    for j in range(2):
        for k in range(4):
            @pl.when(jnp.logical_not((k == x) & (c == xfrom)))
            def _():
                pltpu.make_async_remote_copy(
                    xenc.at[0], xr3.at[k, :, pl.ds(j * 128, 128)],
                    ss.at[X_SUM + 4 * j + k], rs.at[X_SUM + 4 * j + k],
                    device_id=core, device_id_type=MESH,
                ).wait_recv()

    v = decode(xr3[0], W_CODE)
    for k in range(1, 4):
        v = v + decode(xr3[k], W_CODE)
    mine = 2 * (x % 2) + c
    out = v[:, :OUT]
    for k, off in ((1, 96), (2, 64), (3, 160)):
        out = jnp.where(mine == k, pltpu.roll(v, 256 - off, 1)[:, :OUT], out)
    wgrad_ref[...] = out

    for cp in sent:
        cp.wait_send()
    for cp, mine in x_cp:
        @pl.when(jnp.logical_not(mine))
        def _():
            cp.wait_send()


def local(feats, head_weight, text_raw, log_temp, bias):
    rows = feats.shape[0]
    factor = loss_scale / (lax.axis_size("dp") * rows * lax.axis_size("blk"))
    vmem = pltpu.VMEM
    scratch = [
        vmem((F, E), BF16),
        vmem((4 * R, F), BF16),
        vmem((F, 8 * R), BF16),
        vmem((4 * R, E), F32),
        vmem((4 * R, 1), F32),
        vmem((8 * R, E), BF16),
        vmem((R, E), BF16),
        vmem((4 * R, E), BF16),
        vmem((F, H), F32),
        vmem((2, R, 8 * R), BF16),
        vmem((2, R, 4 * R), BF16),
        vmem((4 * R, 4 * R), BF16),
        vmem((2, R, E), F32),
        vmem((R, E), BF16),
        vmem((R, E), BF16),
        vmem((8 * R, H), BF16),
        vmem((4 * R, H), BF16),
        vmem((24, 2 * OUT, 256), BF16),
        vmem((24, 2 * OUT, 256), BF16),
        vmem((2 * OUT, H), F32),
        vmem((2 * OUT, H), BF16),
        vmem((3, 3, OUT, 128), BF16),
        vmem((3, OUT, 128), BF16),
        vmem((4, OUT, 256), BF16),
        vmem((8, 128), F32),
        pltpu.SemaphoreType.DMA((3,)),
        pltpu.SemaphoreType.DMA((N_SEM,)),
        pltpu.SemaphoreType.DMA((N_SEM,)),
    ]
    anyspec = pl.BlockSpec(memory_space=pl.ANY)
    smem = pl.BlockSpec(memory_space=pltpu.SMEM)
    text_grad, weight_grad = pl.pallas_call(
        functools.partial(kernel, factor),
        out_shape=(
            pltpu.VMEM((R, E), F32),
            jax.ShapeDtypeStruct((OUT, OUT), F32),
        ),
        in_specs=[smem, smem, anyspec, anyspec, anyspec],
        out_specs=(pl.BlockSpec(memory_space=pltpu.VMEM), pl.BlockSpec(memory_space=pltpu.VMEM)),
        scratch_shapes=scratch,
        compiler_params=pltpu.CompilerParams(
            collective_id=0, has_side_effects=True, vmem_limit_bytes=59 * 1024 * 1024
        ),
        cost_estimate=pl.CostEstimate(
            flops=20_000_000_000, bytes_accessed=8_000_000, transcendentals=4_000_000
        ),
    )(log_temp, bias, feats, head_weight, text_raw)
    scale = jnp.exp(log_temp[0])
    return scale * text_grad, scale * weight_grad


def solution(mesh):
    return jax.shard_map(
        local,
        mesh=mesh,
        in_specs=(P(("dp", "blk"), None), P(), P(("dp", "blk"), None), P(), P()),
        out_specs=(P(("dp", "blk"), None), P("dp", "blk")),
        check_vma=False,
    )
```
